256 devices in a mesh: tm: 16 (over z, core), row: 16 (over x, y).
Axes of the slice: x: 4, y: 4, z: 8, core: 2. Of those that a mesh axis runs over, the one named last changes fastest.
Arguments:
- hidden_state: bfloat16 [2, 48, 16, 160, 512], P(None, 'tm', 'row'), may hold values from -64 to 64
- grad_out: bfloat16 [2, 48, 16, 160, 512], P(None, 'tm', 'row'), may hold values from -6 to 6
- norm_gain: float32 [512], replicated, may hold values from 0.1 to 1.9
- norm_shift: float32 [512], replicated, may hold values from -4 to 4
- conv_weight: bfloat16 [512, 27, 512], P('row'), may hold values from -0.0546875 to 0.0546875
Outputs:
- grad_hidden: bfloat16 [2, 48, 16, 160, 512], P(None, 'tm', 'row')
The draws below stay inside these ranges and needn't reach their ends.
All inputs are finite; a program needn't handle non-finite values.
Results may differ from the reference program's by a relative error of at most 0.001.
Values may be sent and summed in bfloat16 or wider, within the bound.
A program may use at most 192 MiB of HBM per device.

```python
import jax
import jax.numpy as jnp
from jax import lax

C = 512
GROUPS = 32
WIDTH = 160
CLIPS = 2
FRAMES = 48
ROWS = 16


def draw_hidden_state(key, part):
    key = jax.random.fold_in(key, 11)
    key_base, key_rough, key_offset = jax.random.split(key, 3)
    shape = (CLIPS, FRAMES, ROWS, WIDTH, C)
    frame_pos = jnp.arange(FRAMES, dtype=jnp.float32) / max(FRAMES - 1, 1)
    row_pos = jnp.arange(ROWS, dtype=jnp.float32) / max(ROWS - 1, 1)
    ramp = (3.0 ** frame_pos)[None, :, None, None, None] * (3.0 ** row_pos)[None, None, :, None, None]
    rough = jnp.exp(jax.random.uniform(key_rough, (CLIPS, FRAMES, ROWS, WIDTH, 1), jnp.float32, -0.7, 0.7))
    offset = jnp.clip(jax.random.normal(key_offset, (CLIPS, 1, 1, 1, C), jnp.float32) * 0.5, -1.5, 1.5)
    base = jnp.clip(jax.random.normal(key_base, shape, jnp.float32), -4.0, 4.0)
    value = base * ramp * rough * 0.5 + offset
    return value.astype(jnp.bfloat16)


def levels(own_key, extent, shards, least, high):
    factor_of, own = 1.0, jax.random.fold_in(own_key, 6)
    for dim, blocks in shards:
        steps = jnp.exp(jax.random.uniform(jax.random.fold_in(own, dim), (blocks,), jnp.float32, least / len(shards), high / len(shards)))
        factor_of = factor_of * jnp.repeat(steps, extent[dim] // blocks).reshape([-1 if axis == dim else 1 for axis in range(len(extent))])
    return factor_of


def scatter_about(rng, shape, scale, limit, cuts=(), held_as=jnp.bfloat16):
    values = scale * jax.random.normal(rng, shape, jnp.float32)
    if cuts:
        values = values * levels(rng, shape, cuts, -0.22, 0.18)
    return jnp.clip(values, -limit, limit).astype(held_as)


def setup_inputs(seed: int = 0) -> dict:
    keys = jax.random.split(jax.random.key(seed), 6)
    hidden_state = draw_hidden_state(jax.random.fold_in(keys[5], 71), 0)
    grad_out = scatter_about(keys[1], (CLIPS, FRAMES, ROWS, WIDTH, C), 1.0, 6.0, ((1, 16), (2, 16)))
    norm_gain = jnp.clip(1.0 + 0.18 * jax.random.normal(keys[2], (C,), jnp.float32), 0.1, 1.9)
    norm_shift = scatter_about(keys[3], (C,), 1.0, 4.0, (), jnp.float32)
    conv_weight = scatter_about(keys[4], (C, 27, C), (27 * C) ** -0.5, 0.0546875, ((0, 16),))
    return {"hidden_state": hidden_state, "grad_out": grad_out, "norm_gain": norm_gain, "norm_shift": norm_shift, "conv_weight": conv_weight}


def reference(hidden_state, grad_out, norm_gain, norm_shift, conv_weight):
    hidden_f = hidden_state.astype(jnp.float32)
    clips, frames, rows, width, chan = hidden_f.shape
    per = chan // GROUPS
    count = frames * rows * width * per

    def group_sum(value):
        return lax.optimization_barrier(jnp.sum(value, axis=(1, 2, 3))).reshape(clips, GROUPS, per).sum(-1)

    def spread(stat):
        return jnp.repeat(stat, per, axis=1)[:, None, None, None, :]
    mean = group_sum(hidden_f) / count
    centered = hidden_f - spread(mean)
    variance = group_sum(centered * centered) / count
    rstd = lax.rsqrt(variance + 1e-06)
    normed = centered * spread(rstd)
    pre = normed * norm_gain + norm_shift
    padded = jnp.pad(grad_out, ((0, 0), (0, 2), (1, 1), (1, 1), (0, 0)))
    weight_f = conv_weight.astype(jnp.float32)
    grad_act = jnp.zeros(hidden_f.shape, jnp.float32)
    for kt in range(3):
        for kr in range(3):
            for kw in range(3):
                piece = padded[:, 2 - kt:2 - kt + frames, 2 - kr:2 - kr + rows, 2 - kw:2 - kw + width, :].astype(jnp.float32)
                grad_act = grad_act + jnp.einsum('bfrwo,io->bfrwi', piece, weight_f[:, 9 * kt + 3 * kr + kw, :])
    sig = jax.nn.sigmoid(pre)
    slope = sig * (1.0 + pre * (1.0 - sig))
    grad_pre = grad_act * slope * norm_gain
    first = group_sum(grad_pre) / count
    second = group_sum(grad_pre * normed) / count
    grad_hidden = spread(rstd) * (grad_pre - spread(first) - normed * spread(second))
    return grad_hidden.astype(jnp.bfloat16)
```

```python
import functools

import jax
import jax.numpy as jnp
from jax import lax
from jax.experimental import pallas as pl
from jax.experimental.pallas import tpu as pltpu
from jax.sharding import PartitionSpec as P

GROUPS = 32
MESH = pl.DeviceIdType.MESH
F32 = jnp.float32
ORDER = (3, 5, 4, 0, 2, 1, 6, 8, 7)
Y_FIRST = (True, True, False, True, True, False, True, True, True)
CHUNKS = 9
EPS = 1e-06


def group_total(value, per):
    lane = lax.broadcasted_iota(jnp.int32, value.shape, 1)
    size = value.shape[1]
    step = 1
    while step < per:
        other = jnp.where(
            (lane & step) != 0, pltpu.roll(value, step, 1), pltpu.roll(value, size - step, 1)
        )
        value = value + other
        step *= 2
    return value


def kernel(
    count,
    hid_hbm, cot_hbm, gain_ref, shift_ref, wt_hbm, out_hbm,
    kern, cot, acc, hid, normed, scale, result, local, gathered, moments,
    w_send, w_recv, h_send, h_recv, f_send, f_recv, c_send, c_recv,
    x_send, x_recv, load_sem, out_sem,
):
    tm, row = lax.axis_index("tm"), lax.axis_index("row")
    core = lax.rem(tm, 2)
    px, py = row // 4, lax.rem(row, 4)
    way = 1 - 2 * core
    per = gain_ref.shape[1] // GROUPS
    local_count = 3 * 160 * per

    def wrap(value, size):
        return lax.rem(value + size, size)

    def at_row(value):
        return (tm, wrap(value, 16))

    def at_tm(value):
        return (wrap(value, 16), row)

    def at_xy(x, y):
        return (tm, wrap(x, 4) * 4 + wrap(y, 4))

    partner = (tm + way, row)

    def remote(src, dst, send, recv, target):
        return pltpu.make_async_remote_copy(
            src_ref=src, dst_ref=dst, send_sem=send, recv_sem=recv,
            device_id=target, device_id_type=MESH,
        )

    def along(k, step):
        return at_xy(px, py + step) if Y_FIRST[k] else at_xy(px + step, py)

    def across(k, step):
        return at_xy(px + step, py) if Y_FIRST[k] else at_xy(px, py + step)

    def piece(k, step, half):
        x, y = (px, wrap(py + step, 4)) if Y_FIRST[k] else (wrap(px + step, 4), py)
        return kern.at[:, ORDER[k], x, y, half]

    def block(k, step, half):
        if Y_FIRST[k]:
            return kern.at[:, ORDER[k], wrap(px + step, 4), :, half]
        return kern.at[:, ORDER[k], :, wrap(py + step, 4), half]

    def first_copy(k, slot):
        step = (1, -1, 2)[slot]
        return remote(
            wt_hbm.at[:, ORDER[k], core], piece(k, 0, core),
            w_send.at[k, slot], w_recv.at[k, slot], along(k, step),
        )

    def first_arrival(k, slot):
        step = (1, -1, 2)[slot]
        mine = piece(k, -step, core)
        return remote(mine, mine, w_send.at[k, slot], w_recv.at[k, slot], along(k, step))

    def second_copy(k, slot):
        step = (1, -1)[slot]
        mine = block(k, 0, core)
        return remote(mine, mine, w_send.at[k, 3 + slot], w_recv.at[k, 3 + slot], across(k, step))

    def second_arrival(k, slot):
        step = (1, -1)[slot]
        mine = block(k, -step, core)
        return remote(mine, mine, w_send.at[k, 3 + slot], w_recv.at[k, 3 + slot], across(k, step))

    def onward_copy(k):
        mine = block(k, -way, core)
        return remote(mine, mine, w_send.at[k, 5], w_recv.at[k, 5], across(k, way))

    def onward_arrival(k):
        mine = block(k, 2, core)
        return remote(mine, mine, w_send.at[k, 5], w_recv.at[k, 5], across(k, way))

    def core_copy(k, slot, half):
        mine = block(k, (0, -1, 1, 2)[slot], half)
        return remote(mine, mine, w_send.at[k, 6 + slot], w_recv.at[k, 6 + slot], partner)

    def stage_1(k):
        for slot in (2, 0, 1):
            first_copy(k, slot).start()

    def stage_2(k):
        for slot in range(3):
            first_arrival(k, slot).wait_recv()
        for slot in range(2):
            second_copy(k, slot).start()
        core_copy(k, 0, core).start()

    def stage_3(k):
        for slot in range(2):
            second_arrival(k, slot).wait_recv()
        onward_copy(k).start()
        for slot in range(2):
            core_copy(k, 1 + slot, core).start()

    def stage_4(k):
        onward_arrival(k).wait_recv()
        core_copy(k, 3, core).start()

    def settle(k):
        for slot in range(4):
            core_copy(k, slot, 1 - core).wait_recv()

    def row_copy(side, f, b):
        step = (1, -1)[side]
        return remote(
            cot_hbm.at[b, f, 0], cot.at[2 * side, 2 * f + b],
            h_send.at[side, 2 * f + b], h_recv.at[side, 2 * f + b], at_row(row + step),
        )

    def frame_copy(f, b):
        return remote(
            cot_hbm.at[b, f, 0], cot.at[1, 6 + 2 * f + b],
            f_send.at[2 * f + b], f_recv.at[2 * f + b], at_tm(tm - 1),
        )

    def corner_copy(side):
        return remote(
            cot.at[2 * side, pl.ds(0, 4)], cot.at[2 * side, pl.ds(6, 4)],
            c_send.at[side], c_recv.at[side], at_tm(tm - 1),
        )

    def start_rows(side):
        for f in range(3):
            for b in range(2):
                row_copy(side, f, b).start()

    def finish_rows(side):
        for f in range(3):
            for b in range(2):
                row_copy(side, f, b).wait_recv()

        @pl.when(row == (0, 15)[side])
        def _():
            cot[2 * side, pl.ds(0, 6)] = jnp.zeros((6, 160, 512), cot.dtype)

        corner_copy(side).start()

    def finish_corner(side):
        corner_copy(side).wait_recv()

        @pl.when(tm == 15)
        def _():
            cot[2 * side, pl.ds(6, 4)] = jnp.zeros((4, 160, 512), cot.dtype)

    def finish_frames():
        for f in range(2):
            for b in range(2):
                frame_copy(f, b).wait_recv()

        @pl.when(tm == 15)
        def _():
            cot[1, pl.ds(6, 4)] = jnp.zeros((4, 160, 512), cot.dtype)

    def exchange_copy(e, k):
        if e % 2 == 0:
            me, target = row, at_row(row + k)
        else:
            me, target = tm, at_tm(tm + k)
        return remote(local.at[e], gathered.at[e, me], x_send.at[e, k], x_recv.at[e, me], target)

    def exchange_start(e):
        me = row if e % 2 == 0 else tm
        gathered[e, me] = local[e]

        def body(k, carry):
            exchange_copy(e, k).start()
            return carry

        lax.fori_loop(1, 16, body, 0)

    def exchange_finish(e):
        me = row if e % 2 == 0 else tm

        def body(k, carry):
            other = lax.rem(me + k, 16)
            there = gathered.at[e, other]
            remote(there, there, x_send.at[e, k], x_recv.at[e, other], partner).wait_recv()
            return carry

        lax.fori_loop(1, 16, body, 0)

    def merge(e, each):
        stats = [gathered[e, i] for i in range(16)]
        mean = functools.reduce(jnp.add, [s[0:2] for s in stats]) * (1.0 / 16)
        square = functools.reduce(jnp.add, [s[2:4] for s in stats])
        for s in stats:
            apart = s[0:2] - mean
            square = square + each * (apart * apart)
        return mean, square

    def matmul_chunk(k):
        j = ORDER[k]
        kr, kw = j // 3, j % 3

        def body(m, carry):
            total = None
            for kt in range(3):
                lhs = cot[2 - kr, pl.ds(2 * (2 - kt) + 3 * m, 3)].reshape(480, 512)
                rhs = kern[kt, j].reshape(512, 512)
                part = lax.dot_general(
                    lhs, rhs, (((1,), (1,)), ((), ())), preferred_element_type=F32
                )
                total = part if total is None else total + part
            total = total.reshape(3, 160, 512)
            here = pl.ds(3 * m, 3)
            if k < 3:
                acc[kw, here] = total
            else:
                acc[kw, here] = acc[kw, here] + total
            return carry

        lax.fori_loop(0, 2, body, 0)

    def fold_columns():
        def body(s, carry):
            place = lax.broadcasted_iota(jnp.int32, (160, 512), 0)
            later = jnp.where(place < 159, pltpu.roll(acc[0, s], 159, 0), 0.0)
            earlier = jnp.where(place > 0, pltpu.roll(acc[2, s], 1, 0), 0.0)
            acc[1, s] = acc[1, s] + later + earlier
            return carry

        lax.fori_loop(0, 6, body, 0)

    barrier = pltpu.get_barrier_semaphore()

    def greet(k, carry):
        pl.semaphore_signal(barrier, inc=1, device_id=at_row(row + k), device_id_type=MESH)
        pl.semaphore_signal(barrier, inc=1, device_id=at_tm(tm + k), device_id_type=MESH)
        return carry

    lax.fori_loop(1, 16, greet, 0)

    loads = [
        pltpu.make_async_copy(wt_hbm.at[:, :, core], kern.at[:, :, px, py, core], load_sem.at[0])
    ]
    for f in range(3):
        for b in range(2):
            s = 2 * f + b
            loads.append(
                pltpu.make_async_copy(hid_hbm.at[b, f, 0], hid.at[s], load_sem.at[1 + s])
            )
    for f in range(3):
        for b in range(2):
            s = 2 * f + b
            loads.append(
                pltpu.make_async_copy(cot_hbm.at[b, f, 0], cot.at[1, s], load_sem.at[7 + s])
            )
    for load in loads:
        load.start()

    pl.semaphore_wait(barrier, 30)
    stage_1(0)
    stage_1(1)
    for f in range(2):
        for b in range(2):
            frame_copy(f, b).start()
    start_rows(1)
    for load in loads:
        load.wait()

    def add_up(fn):
        rows = []
        for b in range(2):
            total = None
            for f in range(3):
                part = jnp.sum(fn(2 * f + b, b), axis=0, keepdims=True)
                total = part if total is None else total + part
            rows.append(total)
        return jnp.concatenate(rows, axis=0)

    own_mean = group_total(add_up(lambda s, b: hid[s].astype(F32)), per) * (1.0 / local_count)

    def deviation(s, b):
        apart = hid[s].astype(F32) - own_mean[b : b + 1]
        return apart * apart

    own_square = group_total(add_up(deviation), per)
    local[0, 0:2] = own_mean
    local[0, 2:4] = own_square
    local[0, 4:8] = jnp.zeros((4, 512), F32)
    exchange_start(0)

    def merge_rows():
        exchange_finish(0)
        mean, square = merge(0, float(local_count))
        local[1, 0:2] = mean
        local[1, 2:4] = square
        local[1, 4:8] = jnp.zeros((4, 512), F32)
        exchange_start(1)

    def merge_all():
        exchange_finish(1)
        mean, square = merge(1, float(local_count) * 16)
        rstd = lax.rsqrt(square * (1.0 / count) + EPS)
        moments[0:2] = mean
        moments[2:4] = rstd

    def prepare():
        def body(s, carry):
            b = lax.rem(s, 2)
            mean, rstd = moments[pl.ds(b, 1)], moments[pl.ds(2 + b, 1)]
            unit = (hid[s].astype(F32) - mean) * rstd
            pre = unit * gain_ref[...] + shift_ref[...]
            sig = 1.0 / (1.0 + jnp.exp(-pre))
            normed[s] = unit
            scale[s] = sig * (1.0 + pre * (1.0 - sig)) * gain_ref[...]
            return carry

        lax.fori_loop(0, 6, body, 0)

    for t in range(CHUNKS + 3):
        if t < CHUNKS:
            stage_2(t)
        if t + 2 < CHUNKS:
            stage_1(t + 2)
        if t == 0:
            start_rows(0)
        if 0 <= t - 1 < CHUNKS:
            stage_3(t - 1)
        if 0 <= t - 2 < CHUNKS:
            stage_4(t - 2)
        if t == 2:
            merge_rows()
            finish_frames()
        if t == 3:
            finish_rows(1)
        if t == 4:
            merge_all()
            finish_rows(0)
        if t == 5:
            prepare()
        k = t - 3
        if k >= 0:
            if k == 3:
                finish_corner(1)
            if k == 6:
                finish_corner(0)
            settle(k)
            matmul_chunk(k)
            if k == CHUNKS - 2:
                fold_columns()

    def terms(s, b):
        grad = acc[1, s] * scale[s]
        acc[1, s] = grad
        return grad

    first = add_up(terms)
    second = add_up(lambda s, b: acc[1, s] * normed[s])
    local[2, 0:4] = group_total(jnp.concatenate([first, second], axis=0), per)
    local[2, 4:8] = jnp.zeros((4, 512), F32)
    exchange_start(2)
    exchange_finish(2)
    local[3] = functools.reduce(jnp.add, [gathered[2, i] for i in range(16)])
    exchange_start(3)
    exchange_finish(3)
    means = functools.reduce(jnp.add, [gathered[3, i] for i in range(16)]) * (1.0 / count)

    stores = []
    for s in range(6):
        f, b = s // 2, s % 2
        rstd = moments[2 + b : 3 + b]
        value = rstd * (acc[1, s] - means[b : b + 1] - normed[s] * means[2 + b : 3 + b])
        result[s] = value.astype(result.dtype)
        store = pltpu.make_async_copy(result.at[s], out_hbm.at[b, f, 0], out_sem.at[s])
        store.start()
        stores.append(store)

    for k in range(CHUNKS):
        for slot in range(3):
            first_copy(k, slot).wait_send()
        for slot in range(2):
            second_copy(k, slot).wait_send()
        onward_copy(k).wait_send()
        for slot in range(4):
            core_copy(k, slot, core).wait_send()
    for f in range(3):
        for b in range(2):
            for side in range(2):
                row_copy(side, f, b).wait_send()
            if f < 2:
                frame_copy(f, b).wait_send()
    for side in range(2):
        corner_copy(side).wait_send()

    def sent(k, carry):
        for e in range(4):
            exchange_copy(e, k).wait_send()
        return carry

    lax.fori_loop(1, 16, sent, 0)
    for store in stores:
        store.wait()


def shards(hidden_state, grad_out, norm_gain, norm_shift, conv_weight):
    clips, frames, rows, width, chan = hidden_state.shape
    devices = lax.axis_size("tm") * lax.axis_size("row")
    count = clips * frames * rows * width * chan // clips // GROUPS * devices
    taps = jnp.swapaxes(conv_weight, 0, 1).reshape(3, 9, 2, 16, chan)
    bf16 = jnp.bfloat16
    anywhere = pl.BlockSpec(memory_space=pl.ANY)
    vmem = pl.BlockSpec(memory_space=pltpu.VMEM)
    dma = pltpu.SemaphoreType.DMA
    return pl.pallas_call(
        functools.partial(kernel, count),
        out_shape=jax.ShapeDtypeStruct(hidden_state.shape, bf16),
        in_specs=[anywhere, anywhere, vmem, vmem, anywhere],
        out_specs=anywhere,
        scratch_shapes=[
            pltpu.VMEM((3, 9, 4, 4, 2, 16, chan), bf16),
            pltpu.VMEM((3, 10, width, chan), bf16),
            pltpu.VMEM((3, 6, width, chan), F32),
            pltpu.VMEM((6, width, chan), bf16),
            pltpu.VMEM((6, width, chan), F32),
            pltpu.VMEM((6, width, chan), F32),
            pltpu.VMEM((6, width, chan), bf16),
            pltpu.VMEM((4, 8, chan), F32),
            pltpu.VMEM((4, 16, 8, chan), F32),
            pltpu.VMEM((4, chan), F32),
            dma((CHUNKS, 10)), dma((CHUNKS, 10)),
            dma((2, 6)), dma((2, 6)),
            dma((4,)), dma((4,)),
            dma((2,)), dma((2,)),
            dma((4, 16)), dma((4, 16)),
            dma((13,)), dma((6,)),
        ],
        compiler_params=pltpu.CompilerParams(
            collective_id=0, has_side_effects=True, vmem_limit_bytes=56 << 20
        ),
        name="conv_grad",
    )(hidden_state, grad_out, norm_gain.reshape(1, chan), norm_shift.reshape(1, chan), taps)


def solution(mesh):
    return jax.shard_map(
        shards,
        mesh=mesh,
        in_specs=(
            P(None, "tm", "row", None, None),
            P(None, "tm", "row", None, None),
            P(),
            P(),
            P("row", None, None),
        ),
        out_specs=P(None, "tm", "row", None, None),
        check_vma=False,
    )
```

```python
import functools

import jax
import jax.numpy as jnp
from jax import lax
from jax.experimental import pallas as pl
from jax.experimental.pallas import tpu as pltpu
from jax.sharding import PartitionSpec as P

GROUPS = 32
MESH = pl.DeviceIdType.MESH
F32 = jnp.float32
ITEMS = (
    (1, True, True), (1, False, True), (0, True, True),
    (2, True, True), (0, False, True), (2, False, False),
)
SHARED = tuple(i for i, item in enumerate(ITEMS) if item[1])
EPS = 1e-06


def group_total(value, per):
    lane = lax.broadcasted_iota(jnp.int32, value.shape, 1)
    size = value.shape[1]
    step = 1
    while step < per:
        other = jnp.where(
            (lane & step) != 0, pltpu.roll(value, step, 1), pltpu.roll(value, size - step, 1)
        )
        value = value + other
        step *= 2
    return value


def kernel(
    count,
    hid_hbm, cot_hbm, gain_ref, shift_ref, wt_hbm, out_hbm,
    kern, cot, acc, hid, normed, scale, result, local, gathered, moments,
    w_send, w_recv, z_send, z_recv, h_send, h_recv, f_send, f_recv, c_send, c_recv,
    x_send, x_recv, load_sem, out_sem,
):
    tm, row = lax.axis_index("tm"), lax.axis_index("row")
    core = lax.rem(tm, 2)
    px, py = row // 4, lax.rem(row, 4)
    way = 1 - 2 * core
    odd = lax.rem(tm // 2, 2)
    per = gain_ref.shape[1] // GROUPS
    local_count = 3 * 160 * per

    def wrap(value, size):
        return lax.rem(value + size, size)

    def at_row(value):
        return (tm, wrap(value, 16))

    def at_tm(value):
        return (wrap(value, 16), row)

    def at_xy(x, y):
        return (tm, wrap(x, 4) * 4 + wrap(y, 4))

    partner = (tm + way, row)

    def remote(src, dst, send, recv, target):
        return pltpu.make_async_remote_copy(
            src_ref=src, dst_ref=dst, send_sem=send, recv_sem=recv,
            device_id=target, device_id_type=MESH,
        )

    def tap(k):
        return 3 * ITEMS[k][0] + (2 * odd if ITEMS[k][1] else 1)

    def other_tap(n):
        return 3 * ITEMS[SHARED[n]][0] + 2 - 2 * odd

    def along(k, step):
        return at_xy(px, py + step) if ITEMS[k][2] else at_xy(px + step, py)

    def across(k, step):
        return at_xy(px + step, py) if ITEMS[k][2] else at_xy(px, py + step)

    def piece(k, step, half):
        x, y = (px, wrap(py + step, 4)) if ITEMS[k][2] else (wrap(px + step, 4), py)
        return kern.at[:, tap(k), x, y, half]

    def block(k, step, half, chosen=None):
        chosen = tap(k) if chosen is None else chosen
        if ITEMS[k][2]:
            return kern.at[:, chosen, wrap(px + step, 4), :, half]
        return kern.at[:, chosen, :, wrap(py + step, 4), half]

    def first_copy(k, slot):
        step = (1, -1, 2)[slot]
        return remote(
            wt_hbm.at[:, tap(k), core], piece(k, 0, core),
            w_send.at[k, slot], w_recv.at[k, slot], along(k, step),
        )

    def first_arrival(k, slot):
        step = (1, -1, 2)[slot]
        mine = piece(k, -step, core)
        return remote(mine, mine, w_send.at[k, slot], w_recv.at[k, slot], along(k, step))

    def second_copy(k, slot):
        step = (1, -1)[slot]
        mine = block(k, 0, core)
        return remote(mine, mine, w_send.at[k, 3 + slot], w_recv.at[k, 3 + slot], across(k, step))

    def second_arrival(k, slot):
        step = (1, -1)[slot]
        mine = block(k, -step, core)
        return remote(mine, mine, w_send.at[k, 3 + slot], w_recv.at[k, 3 + slot], across(k, step))

    def onward_copy(k):
        mine = block(k, -way, core)
        return remote(mine, mine, w_send.at[k, 5], w_recv.at[k, 5], across(k, way))

    def onward_arrival(k):
        mine = block(k, 2, core)
        return remote(mine, mine, w_send.at[k, 5], w_recv.at[k, 5], across(k, way))

    STEPS = (0, -1, 1, 2)

    def core_copy(k, slot, half):
        mine = block(k, STEPS[slot], half)
        return remote(mine, mine, w_send.at[k, 6 + slot], w_recv.at[k, 6 + slot], partner)

    def plane_copy(n, slot):
        mine = block(SHARED[n], STEPS[slot], core)
        step = 1 if n == 0 else way
        return remote(mine, mine, z_send.at[n, slot], z_recv.at[n, slot], at_tm(tm + 2 * step))

    def plane_arrival(n, slot):
        mine = block(SHARED[n], STEPS[slot], core, other_tap(n))
        return remote(mine, mine, z_send.at[n, slot], z_recv.at[n, slot], partner)

    def pass_copy(n, slot, half):
        mine = block(SHARED[n], STEPS[slot], half, other_tap(n))
        return remote(mine, mine, z_send.at[n, 4 + slot], z_recv.at[n, 4 + slot], partner)

    def stage_1(k):
        for slot in (2, 0, 1):
            first_copy(k, slot).start()

    def hand_on(k, slot):
        if ITEMS[k][1]:
            plane_copy(SHARED.index(k), slot).start()
        core_copy(k, slot, core).start()

    def stage_2(k):
        for slot in range(3):
            first_arrival(k, slot).wait_recv()
        for slot in range(2):
            second_copy(k, slot).start()
        hand_on(k, 0)

    def stage_3(k):
        for slot in range(2):
            second_arrival(k, slot).wait_recv()
        onward_copy(k).start()
        for slot in range(2):
            hand_on(k, 1 + slot)

    def stage_4(k):
        onward_arrival(k).wait_recv()
        hand_on(k, 3)

    def take_planes(n, slots):
        for slot in slots:
            plane_arrival(n, slot).wait_recv()
            pass_copy(n, slot, core).start()

    def settle(k):
        for slot in range(4):
            core_copy(k, slot, 1 - core).wait_recv()

    def settle_planes(n):
        for slot in range(4):
            pass_copy(n, slot, 1 - core).wait_recv()

    def row_copy(side, f, b):
        step = (1, -1)[side]
        return remote(
            cot_hbm.at[b, f, 0], cot.at[2 * side, 2 * f + b],
            h_send.at[side, 2 * f + b], h_recv.at[side, 2 * f + b], at_row(row + step),
        )

    def frame_copy(f, b):
        return remote(
            cot_hbm.at[b, f, 0], cot.at[1, 6 + 2 * f + b],
            f_send.at[2 * f + b], f_recv.at[2 * f + b], at_tm(tm - 1),
        )

    def corner_copy(side, f):
        return remote(
            cot.at[2 * side, pl.ds(2 * f, 2)], cot.at[2 * side, pl.ds(6 + 2 * f, 2)],
            c_send.at[side, f], c_recv.at[side, f], at_tm(tm - 1),
        )

    def start_rows(f):
        for b in range(2):
            for side in range(2):
                row_copy(side, f, b).start()

    def finish_rows(f):
        for side in range(2):
            for b in range(2):
                row_copy(side, f, b).wait_recv()

            @pl.when(row == (0, 15)[side])
            def _():
                cot[2 * side, pl.ds(2 * f, 2)] = jnp.zeros((2, 160, 512), cot.dtype)

            if f < 2:
                corner_copy(side, f).start()

    def finish_corner(side):
        for f in range(2):
            corner_copy(side, f).wait_recv()

        @pl.when(tm == 15)
        def _():
            cot[2 * side, pl.ds(6, 4)] = jnp.zeros((4, 160, 512), cot.dtype)

    def finish_frames():
        for f in range(2):
            for b in range(2):
                frame_copy(f, b).wait_recv()

        @pl.when(tm == 15)
        def _():
            cot[1, pl.ds(6, 4)] = jnp.zeros((4, 160, 512), cot.dtype)

    def exchange_copy(e, k):
        if e % 2 == 0:
            me, target = row, at_row(row + k)
        else:
            me, target = tm, at_tm(tm + k)
        return remote(local.at[e], gathered.at[e, me], x_send.at[e, k], x_recv.at[e, me], target)

    def exchange_start(e):
        me = row if e % 2 == 0 else tm
        gathered[e, me] = local[e]

        def body(k, carry):
            exchange_copy(e, k).start()
            return carry

        lax.fori_loop(1, 16, body, 0)

    def exchange_finish(e):
        me = row if e % 2 == 0 else tm

        def body(k, carry):
            other = lax.rem(me + k, 16)
            there = gathered.at[e, other]
            remote(there, there, x_send.at[e, k], x_recv.at[e, other], partner).wait_recv()
            return carry

        lax.fori_loop(1, 16, body, 0)

    def merge(e, each):
        stats = [gathered[e, i] for i in range(16)]
        mean = functools.reduce(jnp.add, [s[0:2] for s in stats]) * (1.0 / 16)
        square = functools.reduce(jnp.add, [s[2:4] for s in stats])
        for s in stats:
            apart = s[0:2] - mean
            square = square + each * (apart * apart)
        return mean, square

    def matmul_chunk(kr, kw):
        j = 3 * kr + kw

        def body(m, carry):
            total = None
            for kt in range(3):
                lhs = cot[2 - kr, pl.ds(2 * (2 - kt) + 3 * m, 3)].reshape(480, 512)
                rhs = kern[kt, j].reshape(512, 512)
                part = lax.dot_general(
                    lhs, rhs, (((1,), (1,)), ((), ())), preferred_element_type=F32
                )
                total = part if total is None else total + part
            total = total.reshape(3, 160, 512)
            here = pl.ds(3 * m, 3)
            if kr == 1:
                acc[kw, here] = total
            else:
                acc[kw, here] = acc[kw, here] + total
            return carry

        lax.fori_loop(0, 2, body, 0)

    def fold_columns():
        def body(s, carry):
            place = lax.broadcasted_iota(jnp.int32, (160, 512), 0)
            later = jnp.where(place < 159, pltpu.roll(acc[0, s], 159, 0), 0.0)
            earlier = jnp.where(place > 0, pltpu.roll(acc[2, s], 1, 0), 0.0)
            acc[1, s] = acc[1, s] + later + earlier
            return carry

        lax.fori_loop(0, 6, body, 0)

    barrier = pltpu.get_barrier_semaphore()

    def greet(k, carry):
        pl.semaphore_signal(barrier, inc=1, device_id=at_row(row + k), device_id_type=MESH)
        pl.semaphore_signal(barrier, inc=1, device_id=at_tm(tm + k), device_id_type=MESH)
        return carry

    lax.fori_loop(1, 16, greet, 0)

    loads = [
        pltpu.make_async_copy(wt_hbm.at[:, tap(k), core], piece(k, 0, core), load_sem.at[13 + k])
        for k in range(6)
    ]
    for f in range(3):
        for b in range(2):
            s = 2 * f + b
            loads.append(
                pltpu.make_async_copy(hid_hbm.at[b, f, 0], hid.at[s], load_sem.at[1 + s])
            )
    for f in range(3):
        for b in range(2):
            s = 2 * f + b
            loads.append(
                pltpu.make_async_copy(cot_hbm.at[b, f, 0], cot.at[1, s], load_sem.at[7 + s])
            )
    for load in loads:
        load.start()

    pl.semaphore_wait(barrier, 30)
    stage_1(0)
    stage_1(1)
    for f in range(2):
        for b in range(2):
            frame_copy(f, b).start()
    start_rows(0)
    for load in loads:
        load.wait()

    chan_of = lax.broadcasted_iota(jnp.int32, (512, 128), 0)
    group_of = lax.broadcasted_iota(jnp.int32, (512, 128), 1)
    picks = (chan_of == group_of * per).astype(F32)
    members = (chan_of // per == group_of).astype(F32)

    def compact(value, chosen):
        return jnp.dot(
            value, chosen, precision=lax.Precision.HIGHEST, preferred_element_type=F32
        )

    def spread(value):
        return lax.dot_general(
            value, members, (((1,), (1,)), ((), ())),
            precision=lax.Precision.HIGHEST, preferred_element_type=F32,
        )

    def add_up(fn):
        rows = []
        for b in range(2):
            total = None
            for f in range(3):
                part = jnp.sum(fn(2 * f + b, b), axis=0, keepdims=True)
                total = part if total is None else total + part
            rows.append(total)
        return jnp.concatenate(rows, axis=0)

    own_mean = group_total(add_up(lambda s, b: hid[s].astype(F32)), per) * (1.0 / local_count)

    def deviation(s, b):
        apart = hid[s].astype(F32) - own_mean[b : b + 1]
        return apart * apart

    own_square = group_total(add_up(deviation), per)
    zeros = jnp.zeros((4, own_mean.shape[1]), F32)
    local[0] = compact(jnp.concatenate([own_mean, own_square, zeros], axis=0), picks)
    exchange_start(0)

    def merge_rows():
        exchange_finish(0)
        mean, square = merge(0, float(local_count))
        local[1] = jnp.concatenate([mean, square, jnp.zeros((4, 128), F32)], axis=0)
        exchange_start(1)

    def merge_all():
        exchange_finish(1)
        mean, square = merge(1, float(local_count) * 16)
        rstd = lax.rsqrt(square * (1.0 / count) + EPS)
        both = jnp.concatenate([mean, rstd, jnp.zeros((4, 128), F32)], axis=0)
        moments[...] = spread(both)

    def prepare():
        def body(s, carry):
            b = lax.rem(s, 2)
            mean, rstd = moments[pl.ds(b, 1)], moments[pl.ds(2 + b, 1)]
            unit = (hid[s].astype(F32) - mean) * rstd
            pre = unit * gain_ref[...] + shift_ref[...]
            sig = 1.0 / (1.0 + jnp.exp(-pre))
            normed[s] = unit
            scale[s] = sig * (1.0 + pre * (1.0 - sig)) * gain_ref[...]
            return carry

        lax.fori_loop(0, 6, body, 0)

    def work(k):
        settle(k)
        matmul_chunk(ITEMS[k][0], 2 * odd if ITEMS[k][1] else 1)

    def work_planes(n):
        settle_planes(n)
        matmul_chunk(ITEMS[SHARED[n]][0], 2 - 2 * odd)

    for t in range(10):
        if t < 6:
            stage_2(t)
        if t + 2 < 6:
            stage_1(t + 2)
        if t < 2:
            start_rows(t + 1)
        if 0 <= t - 1 < 6:
            stage_3(t - 1)
        if 0 <= t - 2 < 6:
            stage_4(t - 2)
        for n in range(3):
            late = t - SHARED[n] - 3
            if 0 <= late < 3:
                take_planes(n, ((0,), (1, 2), (3,))[late])
        if t == 2:
            merge_rows()
            finish_rows(0)
        elif t == 3:
            finish_rows(1)
            finish_frames()
            work(0)
        elif t == 4:
            finish_rows(2)
            merge_all()
            work(1)
        elif t == 5:
            prepare()
        elif t == 6:
            work_planes(0)
            finish_corner(1)
            work(2)
        elif t == 7:
            work(4)
            finish_corner(0)
            work(3)
        elif t == 8:
            work_planes(1)
        elif t == 9:
            work_planes(2)
            fold_columns()
            work(5)

    def terms(s, b):
        grad = acc[1, s] * scale[s]
        acc[1, s] = grad
        return grad

    first = add_up(terms)
    second = add_up(lambda s, b: acc[1, s] * normed[s])
    local[2] = compact(jnp.concatenate([first, second, zeros], axis=0), members)
    exchange_start(2)
    exchange_finish(2)
    local[3] = functools.reduce(jnp.add, [gathered[2, i] for i in range(16)])
    exchange_start(3)
    exchange_finish(3)
    totals = functools.reduce(jnp.add, [gathered[3, i] for i in range(16)])
    means = spread(totals * (1.0 / count))

    stores = []
    for s in range(6):
        f, b = s // 2, s % 2
        rstd = moments[2 + b : 3 + b]
        value = rstd * (acc[1, s] - means[b : b + 1] - normed[s] * means[2 + b : 3 + b])
        result[s] = value.astype(result.dtype)
        store = pltpu.make_async_copy(result.at[s], out_hbm.at[b, f, 0], out_sem.at[s])
        store.start()
        stores.append(store)

    for k in range(6):
        for slot in range(3):
            first_copy(k, slot).wait_send()
        for slot in range(2):
            second_copy(k, slot).wait_send()
        onward_copy(k).wait_send()
        for slot in range(4):
            core_copy(k, slot, core).wait_send()
    for n in range(3):
        for slot in range(4):
            plane_copy(n, slot).wait_send()
            pass_copy(n, slot, core).wait_send()
    for f in range(3):
        for side in range(2):
            for b in range(2):
                row_copy(side, f, b).wait_send()
            if f < 2:
                corner_copy(side, f).wait_send()
        if f < 2:
            for b in range(2):
                frame_copy(f, b).wait_send()

    def sent(k, carry):
        for e in range(4):
            exchange_copy(e, k).wait_send()
        return carry

    lax.fori_loop(1, 16, sent, 0)
    for store in stores:
        store.wait()


def shards(hidden_state, grad_out, norm_gain, norm_shift, conv_weight):
    clips, frames, rows, width, chan = hidden_state.shape
    devices = lax.axis_size("tm") * lax.axis_size("row")
    count = clips * frames * rows * width * chan // clips // GROUPS * devices
    taps = jnp.swapaxes(conv_weight, 0, 1).reshape(3, 9, 2, 16, chan)
    bf16 = jnp.bfloat16
    anywhere = pl.BlockSpec(memory_space=pl.ANY)
    vmem = pl.BlockSpec(memory_space=pltpu.VMEM)
    dma = pltpu.SemaphoreType.DMA
    return pl.pallas_call(
        functools.partial(kernel, count),
        out_shape=jax.ShapeDtypeStruct(hidden_state.shape, bf16),
        in_specs=[anywhere, anywhere, vmem, vmem, anywhere],
        out_specs=anywhere,
        scratch_shapes=[
            pltpu.VMEM((3, 9, 4, 4, 2, 16, chan), bf16),
            pltpu.VMEM((3, 10, width, chan), bf16),
            pltpu.VMEM((3, 6, width, chan), F32),
            pltpu.VMEM((6, width, chan), bf16),
            pltpu.VMEM((6, width, chan), F32),
            pltpu.VMEM((6, width, chan), F32),
            pltpu.VMEM((6, width, chan), bf16),
            pltpu.VMEM((4, 8, 128), F32),
            pltpu.VMEM((4, 16, 8, 128), F32),
            pltpu.VMEM((8, chan), F32),
            dma((6, 10)), dma((6, 10)),
            dma((3, 8)), dma((3, 8)),
            dma((2, 6)), dma((2, 6)),
            dma((4,)), dma((4,)),
            dma((2, 2)), dma((2, 2)),
            dma((4, 16)), dma((4, 16)),
            dma((19,)), dma((6,)),
        ],
        compiler_params=pltpu.CompilerParams(
            collective_id=0, has_side_effects=True, vmem_limit_bytes=56 << 20
        ),
        name="conv_grad",
    )(hidden_state, grad_out, norm_gain.reshape(1, chan), norm_shift.reshape(1, chan), taps)


def solution(mesh):
    return jax.shard_map(
        shards,
        mesh=mesh,
        in_specs=(
            P(None, "tm", "row", None, None),
            P(None, "tm", "row", None, None),
            P(),
            P(),
            P("row", None, None),
        ),
        out_specs=P(None, "tm", "row", None, None),
        check_vma=False,
    )
```

```python
import functools

import jax
import jax.numpy as jnp
from jax import lax
from jax.experimental import pallas as pl
from jax.experimental.pallas import tpu as pltpu
from jax.sharding import PartitionSpec as P

GROUPS = 32
MESH = pl.DeviceIdType.MESH
F32 = jnp.float32
ITEMS = ((3, 5, True), (0, 2, False), (6, 8, True), (1, 7, True), (4, 4, False))
SCHEDULE = (
    "F", "A0", "A1", "A2", "A3", "A4", "E", "B0", "H00", "H01", "B1", "C0", "H10", "H11", "J",
    "M", "B2", "C1", "D0", "H20", "H21", "N", "B3", "C2", "D1", "P0", "P1", "P2", "T00", "W00",
    "P3", "W01", "I0", "B4", "C3", "D2", "P4", "T01", "P5", "I1", "T10", "T02", "V00", "V01",
    "C4", "D3", "T11", "I2", "T20", "K1", "W10", "W11", "T12", "K0", "W20", "D4", "T21", "W21",
    "V10", "V11", "T30", "T22", "W30", "W31", "T31", "V20", "V21", "T32", "X", "V30", "V31",
)
SHARED = 4
EPS = 1e-06


def group_total(value, per):
    lane = lax.broadcasted_iota(jnp.int32, value.shape, 1)
    size = value.shape[1]
    step = 1
    while step < per:
        other = jnp.where(
            (lane & step) != 0, pltpu.roll(value, step, 1), pltpu.roll(value, size - step, 1)
        )
        value = value + other
        step *= 2
    return value


def kernel(
    count,
    hid_hbm, cot_hbm, gain_ref, shift_ref, wt_hbm, out_hbm,
    kern, cot, acc, hid, normed, scale, result, local, gathered, moments,
    w_send, w_recv, z_send, z_recv, h_send, h_recv, f_send, f_recv, c_send, c_recv, v_send, v_recv,
    x_send, x_recv, load_sem, out_sem,
):
    tm, row = lax.axis_index("tm"), lax.axis_index("row")
    core = lax.rem(tm, 2)
    px, py = row // 4, lax.rem(row, 4)
    way = 1 - 2 * core
    x_way = jnp.where(py == 3, -1, jnp.where(py == 0, 1, way))
    odd = lax.rem(tm // 2, 2)
    per = gain_ref.shape[1] // GROUPS
    local_count = 3 * 160 * per

    def wrap(value, size):
        return lax.rem(value + size, size)

    def at_row(value):
        return (tm, wrap(value, 16))

    def at_tm(value):
        return (wrap(value, 16), row)

    def at_xy(x, y):
        return (tm, wrap(x, 4) * 4 + wrap(y, 4))

    partner = (tm + way, row)

    def remote(src, dst, send, recv, target):
        return pltpu.make_async_remote_copy(
            src_ref=src, dst_ref=dst, send_sem=send, recv_sem=recv,
            device_id=target, device_id_type=MESH,
        )

    def tap(k):
        even, other, _ = ITEMS[k]
        return even + odd * (other - even)

    def other_tap(n):
        even, other, _ = ITEMS[n]
        return other + odd * (even - other)

    def along(k, step):
        return at_xy(px, py + step) if ITEMS[k][2] else at_xy(px + step, py)

    def across(k, step):
        return at_xy(px + step, py) if ITEMS[k][2] else at_xy(px, py + step)

    def piece(k, step, half):
        x, y = (px, wrap(py + step, 4)) if ITEMS[k][2] else (wrap(px + step, 4), py)
        return kern.at[:, tap(k), x, y, half]

    def block(k, step, half, chosen=None):
        chosen = tap(k) if chosen is None else chosen
        if ITEMS[k][2]:
            return kern.at[:, chosen, wrap(px + step, 4), :, half]
        return kern.at[:, chosen, :, wrap(py + step, 4), half]

    def first_copy(k, slot):
        step = (1, -1, 2)[slot]
        return remote(
            wt_hbm.at[:, tap(k), core], piece(k, 0, core),
            w_send.at[k, slot], w_recv.at[k, slot], along(k, step),
        )

    def first_arrival(k, slot):
        step = (1, -1, 2)[slot]
        mine = piece(k, -step, core)
        return remote(mine, mine, w_send.at[k, slot], w_recv.at[k, slot], along(k, step))

    def second_copy(k, slot):
        step = (1, -1)[slot]
        mine = block(k, 0, core)
        return remote(mine, mine, w_send.at[k, 3 + slot], w_recv.at[k, 3 + slot], across(k, step))

    def second_arrival(k, slot):
        step = (1, -1)[slot]
        mine = block(k, -step, core)
        return remote(mine, mine, w_send.at[k, 3 + slot], w_recv.at[k, 3 + slot], across(k, step))

    def onward_copy(k):
        step = x_way if ITEMS[k][2] else way
        mine = block(k, -step, core)
        return remote(mine, mine, w_send.at[k, 5], w_recv.at[k, 5], across(k, step))

    def onward_arrival(k):
        mine = block(k, 2, core)
        return remote(mine, mine, w_send.at[k, 5], w_recv.at[k, 5], across(k, way))

    STEPS = (0, -1, 1, 2)

    def core_copy(k, slot, half):
        mine = block(k, STEPS[slot], half)
        return remote(mine, mine, w_send.at[k, 6 + slot], w_recv.at[k, 6 + slot], partner)

    def share(n, slot, end, chosen=None):
        k = n
        chosen = tap(k) if chosen is None else chosen
        there = pl.ds(2 * end, 2)
        if ITEMS[k][2]:
            return kern.at[:, chosen, wrap(px + STEPS[slot], 4), there, core]
        return kern.at[:, chosen, there, wrap(py + STEPS[slot], 4), core]

    def plane_copy(n, slot, end):
        mine = share(n, slot, end)
        return remote(
            mine, mine, z_send.at[n, slot, end], z_recv.at[n, slot, end],
            at_tm(tm + (2, -2)[end]),
        )

    def plane_arrival(n, slot, end):
        mine = share(n, slot, end, other_tap(n))
        return remote(mine, mine, z_send.at[n, slot, end], z_recv.at[n, slot, end], partner)

    def pass_copy(n, slot, half):
        mine = block(n, STEPS[slot], half, other_tap(n))
        return remote(mine, mine, z_send.at[n, slot, 2], z_recv.at[n, slot, 2], partner)

    def stage_1(k):
        for slot in (2, 0, 1):
            first_copy(k, slot).start()

    def hand_on(k, slot):
        if k < SHARED:
            for end in range(2):
                plane_copy(k, slot, end).start()
        core_copy(k, slot, core).start()

    def stage_2(k):
        for slot in range(3):
            first_arrival(k, slot).wait_recv()
        for slot in range(2):
            second_copy(k, slot).start()
        hand_on(k, 0)

    def stage_3(k):
        for slot in range(2):
            second_arrival(k, slot).wait_recv()
        onward_copy(k).start()
        for slot in range(2):
            hand_on(k, 1 + slot)

    def stage_4(k):
        onward_arrival(k).wait_recv()
        hand_on(k, 3)

    def take_planes(n, part):
        for slot in ((0,), (1, 2), (3,))[part]:
            for end in range(2):
                plane_arrival(n, slot, end).wait_recv()
            pass_copy(n, slot, core).start()

    def settle(k):
        for slot in range(4):
            core_copy(k, slot, 1 - core).wait_recv()

    def settle_planes(n):
        for slot in range(4):
            pass_copy(n, slot, 1 - core).wait_recv()

    def row_copy(side, f, b):
        step = (1, -1)[side]
        return remote(
            cot_hbm.at[b, f, 0], cot.at[2 * side, 2 * f + b],
            h_send.at[side, 2 * f + b], h_recv.at[side, 2 * f + b], at_row(row + step),
        )

    def frame_copy(f, b):
        return remote(
            cot_hbm.at[b, f, 0], cot.at[1, 6 + 2 * f + b],
            f_send.at[2 * f + b], f_recv.at[2 * f + b], at_tm(tm - 1),
        )

    def corner_copy(side, f):
        return remote(
            cot.at[2 * side, pl.ds(2 * f, 2)], cot.at[2 * side, pl.ds(6 + 2 * f, 2)],
            c_send.at[side, f], c_recv.at[side, f], partner,
        )

    def wing_copy(side):
        return remote(
            cot.at[1, pl.ds(6, 4)], cot.at[2 * side, pl.ds(6, 4)],
            v_send.at[side], v_recv.at[side], at_row(row + (1, -1)[side]),
        )

    def start_rows(f, b):
        for side in range(2):
            row_copy(side, f, b).start()

    def finish_rows(f):
        for side in range(2):
            for b in range(2):
                row_copy(side, f, b).wait_recv()

            @pl.when(row == (0, 15)[side])
            def _():
                cot[2 * side, pl.ds(2 * f, 2)] = jnp.zeros((2, 160, 512), cot.dtype)

            if f < 2:

                @pl.when(core == 1)
                def _():
                    corner_copy(side, f).start()

    def finish_corner(side):
        @pl.when(core == 0)
        def _():
            for f in range(2):
                corner_copy(side, f).wait_recv()

        @pl.when(core == 1)
        def _():
            wing_copy(side).wait_recv()

        @pl.when(row == (0, 15)[side])
        def _():
            cot[2 * side, pl.ds(6, 4)] = jnp.zeros((4, 160, 512), cot.dtype)

    def finish_frames():
        for f in range(2):
            for b in range(2):
                frame_copy(f, b).wait_recv()

        @pl.when(tm == 15)
        def _():
            cot[1, pl.ds(6, 4)] = jnp.zeros((4, 160, 512), cot.dtype)

        @pl.when(core == 1)
        def _():
            for side in range(2):
                wing_copy(side).start()

    def exchange_copy(e, k):
        if e % 2 == 0:
            me, target = row, at_row(row + k)
        else:
            me, target = tm, at_tm(tm + k)
        return remote(local.at[e], gathered.at[e, me], x_send.at[e, k], x_recv.at[e, me], target)

    def exchange_start(e):
        me = row if e % 2 == 0 else tm
        gathered[e, me] = local[e]

        def body(k, carry):
            exchange_copy(e, k).start()
            return carry

        lax.fori_loop(1, 16, body, 0)

    def exchange_finish(e):
        me = row if e % 2 == 0 else tm

        def body(k, carry):
            other = lax.rem(me + k, 16)
            there = gathered.at[e, other]
            remote(there, there, x_send.at[e, k], x_recv.at[e, other], partner).wait_recv()
            return carry

        lax.fori_loop(1, 16, body, 0)

    def merge(e, each):
        stats = [gathered[e, i] for i in range(16)]
        mean = functools.reduce(jnp.add, [s[0:2] for s in stats]) * (1.0 / 16)
        square = functools.reduce(jnp.add, [s[2:4] for s in stats])
        for s in stats:
            apart = s[0:2] - mean
            square = square + each * (apart * apart)
        return mean, square

    def product(m, kr, kw):
        total = None
        for kt in range(3):
            lhs = cot[2 - kr, pl.ds(2 * (2 - kt) + 3 * m, 3)].reshape(480, 512)
            rhs = kern[kt, 3 * kr + kw].reshape(512, 512)
            part = lax.dot_general(
                lhs, rhs, (((1,), (1,)), ((), ())), preferred_element_type=F32
            )
            total = part if total is None else total + part
        return total.reshape(3, 160, 512)

    def matmul_half(m, kr, kw):
        here = pl.ds(3 * m, 3)
        acc[kw, here] = acc[kw, here] + product(m, kr, kw)

    def fold_columns():
        def body(s, carry):
            place = lax.broadcasted_iota(jnp.int32, (160, 512), 0)
            later = jnp.where(place < 159, pltpu.roll(acc[0, s], 159, 0), 0.0)
            earlier = jnp.where(place > 0, pltpu.roll(acc[2, s], 1, 0), 0.0)
            acc[1, s] = acc[1, s] + later + earlier
            return carry

        lax.fori_loop(0, 6, body, 0)

    barrier = pltpu.get_barrier_semaphore()

    def greet(k, carry):
        pl.semaphore_signal(barrier, inc=1, device_id=at_row(row + k), device_id_type=MESH)
        pl.semaphore_signal(barrier, inc=1, device_id=at_tm(tm + k), device_id_type=MESH)
        return carry

    lax.fori_loop(1, 16, greet, 0)

    loads = [
        pltpu.make_async_copy(wt_hbm.at[:, tap(k), core], piece(k, 0, core), load_sem.at[13 + k])
        for k in range(5)
    ]
    for f in range(3):
        for b in range(2):
            s = 2 * f + b
            loads.append(
                pltpu.make_async_copy(hid_hbm.at[b, f, 0], hid.at[s], load_sem.at[1 + s])
            )
    for f in range(3):
        for b in range(2):
            s = 2 * f + b
            loads.append(
                pltpu.make_async_copy(cot_hbm.at[b, f, 0], cot.at[1, s], load_sem.at[7 + s])
            )
    for load in loads:
        load.start()
    acc[...] = jnp.zeros_like(acc)

    for load in loads[5:11]:
        load.wait()

    chan_of = lax.broadcasted_iota(jnp.int32, (512, 128), 0)
    group_of = lax.broadcasted_iota(jnp.int32, (512, 128), 1)
    picks = (chan_of == group_of * per).astype(F32)
    members = (chan_of // per == group_of).astype(F32)

    def compact(value, chosen):
        return jnp.dot(
            value, chosen, precision=lax.Precision.HIGHEST, preferred_element_type=F32
        )

    def spread(value):
        return lax.dot_general(
            value, members, (((1,), (1,)), ((), ())),
            precision=lax.Precision.HIGHEST, preferred_element_type=F32,
        )

    def add_up(fn):
        rows = []
        for b in range(2):
            total = None
            for f in range(3):
                part = jnp.sum(fn(2 * f + b, b), axis=0, keepdims=True)
                total = part if total is None else total + part
            rows.append(total)
        return jnp.concatenate(rows, axis=0)

    own_mean = group_total(add_up(lambda s, b: hid[s].astype(F32)), per) * (1.0 / local_count)

    def deviation(s, b):
        apart = hid[s].astype(F32) - own_mean[b : b + 1]
        return apart * apart

    own_square = group_total(add_up(deviation), per)
    zeros = jnp.zeros((4, own_mean.shape[1]), F32)
    local[0] = compact(jnp.concatenate([own_mean, own_square, zeros], axis=0), picks)
    pl.semaphore_wait(barrier, 30)
    for load in loads[:5] + loads[11:]:
        load.wait()
    def merge_rows():
        exchange_finish(0)
        mean, square = merge(0, float(local_count))
        local[1] = jnp.concatenate([mean, square, jnp.zeros((4, 128), F32)], axis=0)
        exchange_start(1)

    def merge_all():
        exchange_finish(1)
        mean, square = merge(1, float(local_count) * 16)
        rstd = lax.rsqrt(square * (1.0 / count) + EPS)
        both = jnp.concatenate([mean, rstd, jnp.zeros((4, 128), F32)], axis=0)
        moments[...] = spread(both)

    def prepare(s):
        b = s % 2
        mean, rstd = moments[b : b + 1], moments[2 + b : 3 + b]
        unit = (hid[s].astype(F32) - mean) * rstd
        pre = unit * gain_ref[...] + shift_ref[...]
        sig = 1.0 / (1.0 + jnp.exp(-pre))
        normed[s] = unit
        scale[s] = sig * (1.0 + pre * (1.0 - sig)) * gain_ref[...]

    def start_frames():
        for f in range(2):
            for b in range(2):
                frame_copy(f, b).start()

    def start_stats():
        exchange_start(0)

    def work(k, m):
        if m == 0:
            settle(k)
        matmul_half(m, tap(k) // 3, lax.rem(tap(k), 3))

    def work_planes(n, m):
        if m == 0:
            settle_planes(n)
        matmul_half(m, other_tap(n) // 3, lax.rem(other_tap(n), 3))

    steps = {
        "A": stage_1, "B": stage_2, "C": stage_3, "D": stage_4, "T": take_planes,
        "F": start_frames, "H": start_rows, "I": finish_rows, "J": finish_frames,
        "K": finish_corner, "E": start_stats, "M": merge_rows, "N": merge_all, "P": prepare,
        "W": work, "V": work_planes, "X": fold_columns,
    }
    for step in SCHEDULE:
        steps[step[0]](*(int(digit) for digit in step[1:]))
    settle(4)

    sums = [[None, None], [None, None]]
    for m in range(2):
        whole = acc[1, 3 * m : 3 * m + 3] + product(m, 1, 1)
        for i in range(3):
            s = 3 * m + i
            grad = whole[i] * scale[s]
            acc[1, s] = grad
            for kind, value in enumerate((grad, grad * normed[s])):
                part = jnp.sum(value, axis=0, keepdims=True)
                held = sums[kind][s % 2]
                sums[kind][s % 2] = part if held is None else held + part
    first, second = (jnp.concatenate(pair, axis=0) for pair in sums)
    local[2] = compact(jnp.concatenate([first, second, zeros], axis=0), members)
    exchange_start(2)

    for k in range(5):
        for slot in range(3):
            first_copy(k, slot).wait_send()
        for slot in range(2):
            second_copy(k, slot).wait_send()
        onward_copy(k).wait_send()
        for slot in range(4):
            core_copy(k, slot, core).wait_send()
    for n in range(SHARED):
        for slot in range(4):
            for end in range(2):
                plane_copy(n, slot, end).wait_send()
            pass_copy(n, slot, core).wait_send()
    @pl.when(core == 1)
    def _():
        for side in range(2):
            wing_copy(side).wait_send()
            for f in range(2):
                corner_copy(side, f).wait_send()

    for f in range(3):
        for side in range(2):
            for b in range(2):
                row_copy(side, f, b).wait_send()
        if f < 2:
            for b in range(2):
                frame_copy(f, b).wait_send()

    exchange_finish(2)
    local[3] = functools.reduce(jnp.add, [gathered[2, i] for i in range(16)])
    exchange_start(3)

    def sent(k, carry):
        for e in range(4):
            exchange_copy(e, k).wait_send()
        return carry

    lax.fori_loop(1, 16, sent, 0)
    exchange_finish(3)
    totals = functools.reduce(jnp.add, [gathered[3, i] for i in range(16)])
    means = spread(totals * (1.0 / count))

    stores = []
    for s in range(6):
        f, b = s // 2, s % 2
        rstd = moments[2 + b : 3 + b]
        low, slope = rstd * means[b : b + 1], rstd * means[2 + b : 3 + b]
        value = rstd * acc[1, s] - low - normed[s] * slope
        result[s] = value.astype(result.dtype)
        store = pltpu.make_async_copy(result.at[s], out_hbm.at[b, f, 0], out_sem.at[s])
        store.start()
        stores.append(store)

    for store in stores:
        store.wait()


def shards(hidden_state, grad_out, norm_gain, norm_shift, conv_weight):
    clips, frames, rows, width, chan = hidden_state.shape
    devices = lax.axis_size("tm") * lax.axis_size("row")
    count = clips * frames * rows * width * chan // clips // GROUPS * devices
    taps = jnp.swapaxes(conv_weight, 0, 1).reshape(3, 9, 2, 16, chan)
    bf16 = jnp.bfloat16
    anywhere = pl.BlockSpec(memory_space=pl.ANY)
    vmem = pl.BlockSpec(memory_space=pltpu.VMEM)
    dma = pltpu.SemaphoreType.DMA
    return pl.pallas_call(
        functools.partial(kernel, count),
        out_shape=jax.ShapeDtypeStruct(hidden_state.shape, bf16),
        in_specs=[anywhere, anywhere, vmem, vmem, anywhere],
        out_specs=anywhere,
        scratch_shapes=[
            pltpu.VMEM((3, 9, 4, 4, 2, 16, chan), bf16),
            pltpu.VMEM((3, 10, width, chan), bf16),
            pltpu.VMEM((3, 6, width, chan), F32),
            pltpu.VMEM((6, width, chan), bf16),
            pltpu.VMEM((6, width, chan), F32),
            pltpu.VMEM((6, width, chan), F32),
            pltpu.VMEM((6, width, chan), bf16),
            pltpu.VMEM((4, 8, 128), F32),
            pltpu.VMEM((4, 16, 8, 128), F32),
            pltpu.VMEM((8, chan), F32),
            dma((5, 10)), dma((5, 10)),
            dma((4, 4, 3)), dma((4, 4, 3)),
            dma((2, 6)), dma((2, 6)),
            dma((4,)), dma((4,)),
            dma((2, 2)), dma((2, 2)),
            dma((2,)), dma((2,)),
            dma((4, 16)), dma((4, 16)),
            dma((18,)), dma((6,)),
        ],
        compiler_params=pltpu.CompilerParams(
            collective_id=0, has_side_effects=True, vmem_limit_bytes=56 << 20
        ),
        name="conv_grad",
    )(hidden_state, grad_out, norm_gain.reshape(1, chan), norm_shift.reshape(1, chan), taps)


def solution(mesh):
    return jax.shard_map(
        shards,
        mesh=mesh,
        in_specs=(
            P(None, "tm", "row", None, None),
            P(None, "tm", "row", None, None),
            P(),
            P(),
            P("row", None, None),
        ),
        out_specs=P(None, "tm", "row", None, None),
        check_vma=False,
    )
```

```python
import functools

import jax
import jax.numpy as jnp
from jax import lax
from jax.experimental import pallas as pl
from jax.experimental.pallas import tpu as pltpu
from jax.sharding import PartitionSpec as P

GROUPS = 32
MESH = pl.DeviceIdType.MESH
F32 = jnp.float32
ITEMS = ((3, 5, True), (0, 2, False), (6, 8, True), (1, 7, True), (4, 4, False))
SCHEDULE = (
    "F", "A0", "A1", "A2", "A3", "A4", "E", "B0", "H00", "B1", "C0", "H01", "H10", "J", "M",
    "B2", "C1", "D0", "H11", "H20", "N", "B3", "C2", "D1", "H21", "P0", "P1", "P2", "T00",
    "W00", "P3", "W01", "I0", "I1", "B4", "C3", "D2", "P4", "T01", "P5", "T10", "T02", "V00",
    "V01", "C4", "D3", "T11", "I2", "K1", "W10", "W11", "T20", "T12", "K0", "W20", "W21", "D4",
    "T30", "T21", "V10", "T22", "V11", "W30", "T31", "W31", "V20", "T32", "V21", "X", "V30",
    "V31",
)
SHARED = 4
EPS = 1e-06


def group_total(value, per):
    lane = lax.broadcasted_iota(jnp.int32, value.shape, 1)
    size = value.shape[1]
    step = 1
    while step < per:
        other = jnp.where(
            (lane & step) != 0, pltpu.roll(value, step, 1), pltpu.roll(value, size - step, 1)
        )
        value = value + other
        step *= 2
    return value


def kernel(
    count,
    hid_hbm, cot_hbm, gain_ref, shift_ref, wt_hbm, out_hbm,
    kern, cot, acc, hid, normed, scale, result, local, gathered, moments,
    w_send, w_recv, z_send, z_recv, h_send, h_recv, f_send, f_recv, c_send, c_recv, v_send, v_recv,
    x_send, x_recv, load_sem, out_sem,
):
    tm, row = lax.axis_index("tm"), lax.axis_index("row")
    core = lax.rem(tm, 2)
    px, py = row // 4, lax.rem(row, 4)
    way = 1 - 2 * core
    x_way = jnp.where(py == 3, -1, jnp.where(py == 0, 1, way))
    odd = lax.rem(tm // 2, 2)
    per = gain_ref.shape[1] // GROUPS
    local_count = 3 * 160 * per

    def wrap(value, size):
        return lax.rem(value + size, size)

    def at_row(value):
        return (tm, wrap(value, 16))

    def at_tm(value):
        return (wrap(value, 16), row)

    def at_xy(x, y):
        return (tm, wrap(x, 4) * 4 + wrap(y, 4))

    partner = (tm + way, row)

    def remote(src, dst, send, recv, target):
        return pltpu.make_async_remote_copy(
            src_ref=src, dst_ref=dst, send_sem=send, recv_sem=recv,
            device_id=target, device_id_type=MESH,
        )

    def tap(k):
        even, other, _ = ITEMS[k]
        return even + odd * (other - even)

    def other_tap(n):
        even, other, _ = ITEMS[n]
        return other + odd * (even - other)

    def along(k, step):
        return at_xy(px, py + step) if ITEMS[k][2] else at_xy(px + step, py)

    def across(k, step):
        return at_xy(px + step, py) if ITEMS[k][2] else at_xy(px, py + step)

    def piece(k, step, half):
        x, y = (px, wrap(py + step, 4)) if ITEMS[k][2] else (wrap(px + step, 4), py)
        return kern.at[:, tap(k), x, y, half]

    def block(k, step, half, chosen=None):
        chosen = tap(k) if chosen is None else chosen
        if ITEMS[k][2]:
            return kern.at[:, chosen, wrap(px + step, 4), :, half]
        return kern.at[:, chosen, :, wrap(py + step, 4), half]

    def first_copy(k, slot):
        step = (1, -1, 2)[slot]
        return remote(
            wt_hbm.at[:, tap(k), core], piece(k, 0, core),
            w_send.at[k, slot], w_recv.at[k, slot], along(k, step),
        )

    def first_arrival(k, slot):
        step = (1, -1, 2)[slot]
        mine = piece(k, -step, core)
        return remote(mine, mine, w_send.at[k, slot], w_recv.at[k, slot], along(k, step))

    def second_copy(k, slot):
        step = (1, -1)[slot]
        mine = block(k, 0, core)
        return remote(mine, mine, w_send.at[k, 3 + slot], w_recv.at[k, 3 + slot], across(k, step))

    def second_arrival(k, slot):
        step = (1, -1)[slot]
        mine = block(k, -step, core)
        return remote(mine, mine, w_send.at[k, 3 + slot], w_recv.at[k, 3 + slot], across(k, step))

    def onward_copy(k):
        step = x_way if ITEMS[k][2] else way
        mine = block(k, -step, core)
        return remote(mine, mine, w_send.at[k, 5], w_recv.at[k, 5], across(k, step))

    def onward_arrival(k):
        mine = block(k, 2, core)
        return remote(mine, mine, w_send.at[k, 5], w_recv.at[k, 5], across(k, way))

    STEPS = (0, -1, 1, 2)

    def core_copy(k, slot, half):
        mine = block(k, STEPS[slot], half)
        return remote(mine, mine, w_send.at[k, 6 + slot], w_recv.at[k, 6 + slot], partner)

    def share(n, slot, end, chosen=None):
        k = n
        chosen = tap(k) if chosen is None else chosen
        there = pl.ds(2 * end, 2)
        if ITEMS[k][2]:
            return kern.at[:, chosen, wrap(px + STEPS[slot], 4), there, core]
        return kern.at[:, chosen, there, wrap(py + STEPS[slot], 4), core]

    def plane_copy(n, slot, end):
        mine = share(n, slot, end)
        return remote(
            mine, mine, z_send.at[n, slot, end], z_recv.at[n, slot, end],
            at_tm(tm + (2, -2)[end]),
        )

    def plane_arrival(n, slot, end):
        mine = share(n, slot, end, other_tap(n))
        return remote(mine, mine, z_send.at[n, slot, end], z_recv.at[n, slot, end], partner)

    def pass_copy(n, slot, half):
        mine = block(n, STEPS[slot], half, other_tap(n))
        return remote(mine, mine, z_send.at[n, slot, 2], z_recv.at[n, slot, 2], partner)

    def stage_1(k):
        for slot in (2, 0, 1):
            first_copy(k, slot).start()

    def hand_on(k, slot):
        if k < SHARED:
            for end in range(2):
                plane_copy(k, slot, end).start()
        core_copy(k, slot, core).start()

    def stage_2(k):
        for slot in range(3):
            first_arrival(k, slot).wait_recv()
        for slot in range(2):
            second_copy(k, slot).start()
        hand_on(k, 0)

    def stage_3(k):
        for slot in range(2):
            second_arrival(k, slot).wait_recv()
        onward_copy(k).start()
        for slot in range(2):
            hand_on(k, 1 + slot)

    def stage_4(k):
        onward_arrival(k).wait_recv()
        hand_on(k, 3)

    def take_planes(n, part):
        for slot in ((0,), (1, 2), (3,))[part]:
            for end in range(2):
                plane_arrival(n, slot, end).wait_recv()
            pass_copy(n, slot, core).start()

    def settle(k):
        for slot in range(4):
            core_copy(k, slot, 1 - core).wait_recv()

    def settle_planes(n):
        for slot in range(4):
            pass_copy(n, slot, 1 - core).wait_recv()

    def row_copy(side, f, b):
        step = (1, -1)[side]
        return remote(
            cot_hbm.at[b, f, 0], cot.at[2 * side, 2 * f + b],
            h_send.at[side, 2 * f + b], h_recv.at[side, 2 * f + b], at_row(row + step),
        )

    def frame_copy(f, b):
        return remote(
            cot_hbm.at[b, f, 0], cot.at[1, 6 + 2 * f + b],
            f_send.at[2 * f + b], f_recv.at[2 * f + b], at_tm(tm - 1),
        )

    def corner_copy(side, f):
        return remote(
            cot.at[2 * side, pl.ds(2 * f, 2)], cot.at[2 * side, pl.ds(6 + 2 * f, 2)],
            c_send.at[side, f], c_recv.at[side, f], partner,
        )

    def wing_copy(side):
        return remote(
            cot.at[1, pl.ds(6, 4)], cot.at[2 * side, pl.ds(6, 4)],
            v_send.at[side], v_recv.at[side], at_row(row + (1, -1)[side]),
        )

    def start_rows(f, b):
        for side in range(2):
            row_copy(side, f, b).start()

    def finish_rows(f):
        for side in range(2):
            for b in range(2):
                row_copy(side, f, b).wait_recv()

            @pl.when(row == (0, 15)[side])
            def _():
                cot[2 * side, pl.ds(2 * f, 2)] = jnp.zeros((2, 160, 512), cot.dtype)

            if f < 2:

                @pl.when(core == 1)
                def _():
                    corner_copy(side, f).start()

    def finish_corner(side):
        @pl.when(core == 0)
        def _():
            for f in range(2):
                corner_copy(side, f).wait_recv()

        @pl.when(core == 1)
        def _():
            wing_copy(side).wait_recv()

        @pl.when(row == (0, 15)[side])
        def _():
            cot[2 * side, pl.ds(6, 4)] = jnp.zeros((4, 160, 512), cot.dtype)

    def finish_frames():
        for f in range(2):
            for b in range(2):
                frame_copy(f, b).wait_recv()

        @pl.when(tm == 15)
        def _():
            cot[1, pl.ds(6, 4)] = jnp.zeros((4, 160, 512), cot.dtype)

        @pl.when(core == 1)
        def _():
            for side in range(2):
                wing_copy(side).start()

    def exchange_copy(e, k):
        if e % 2 == 0:
            me, target = row, at_row(row + k)
        else:
            me, target = tm, at_tm(tm + k)
        return remote(local.at[e], gathered.at[e, me], x_send.at[e, k], x_recv.at[e, me], target)

    def exchange_start(e):
        me = row if e % 2 == 0 else tm
        gathered[e, me] = local[e]

        def body(k, carry):
            exchange_copy(e, k).start()
            return carry

        lax.fori_loop(1, 16, body, 0)

    def exchange_finish(e):
        me = row if e % 2 == 0 else tm

        def body(k, carry):
            other = lax.rem(me + k, 16)
            there = gathered.at[e, other]
            remote(there, there, x_send.at[e, k], x_recv.at[e, other], partner).wait_recv()
            return carry

        lax.fori_loop(1, 16, body, 0)

    def merge(e, each):
        stats = [gathered[e, i] for i in range(16)]
        mean = functools.reduce(jnp.add, [s[0:2] for s in stats]) * (1.0 / 16)
        square = functools.reduce(jnp.add, [s[2:4] for s in stats])
        for s in stats:
            apart = s[0:2] - mean
            square = square + each * (apart * apart)
        return mean, square

    def product(m, kr, kw):
        total = None
        for kt in range(3):
            lhs = cot[2 - kr, pl.ds(2 * (2 - kt) + 3 * m, 3)].reshape(480, 512)
            rhs = kern[kt, 3 * kr + kw].reshape(512, 512)
            part = lax.dot_general(
                lhs, rhs, (((1,), (1,)), ((), ())), preferred_element_type=F32
            )
            total = part if total is None else total + part
        return total.reshape(3, 160, 512)

    def matmul_half(m, kr, kw):
        here = pl.ds(3 * m, 3)
        acc[kw, here] = acc[kw, here] + product(m, kr, kw)

    def fold_columns():
        def body(s, carry):
            place = lax.broadcasted_iota(jnp.int32, (160, 512), 0)
            later = jnp.where(place < 159, pltpu.roll(acc[0, s], 159, 0), 0.0)
            earlier = jnp.where(place > 0, pltpu.roll(acc[2, s], 1, 0), 0.0)
            acc[1, s] = acc[1, s] + later + earlier
            return carry

        lax.fori_loop(0, 6, body, 0)

    barrier = pltpu.get_barrier_semaphore()

    def greet(k, carry):
        pl.semaphore_signal(barrier, inc=1, device_id=at_row(row + k), device_id_type=MESH)
        pl.semaphore_signal(barrier, inc=1, device_id=at_tm(tm + k), device_id_type=MESH)
        return carry

    lax.fori_loop(1, 16, greet, 0)

    loads = [
        pltpu.make_async_copy(wt_hbm.at[:, tap(k), core], piece(k, 0, core), load_sem.at[13 + k])
        for k in range(5)
    ]
    for f in range(3):
        for b in range(2):
            s = 2 * f + b
            loads.append(
                pltpu.make_async_copy(hid_hbm.at[b, f, 0], hid.at[s], load_sem.at[1 + s])
            )
    for f in range(3):
        for b in range(2):
            s = 2 * f + b
            loads.append(
                pltpu.make_async_copy(cot_hbm.at[b, f, 0], cot.at[1, s], load_sem.at[7 + s])
            )
    for load in loads:
        load.start()
    acc[...] = jnp.zeros_like(acc)

    for load in loads[5:11]:
        load.wait()

    chan_of = lax.broadcasted_iota(jnp.int32, (512, 128), 0)
    group_of = lax.broadcasted_iota(jnp.int32, (512, 128), 1)
    picks = (chan_of == group_of * per).astype(F32)
    members = (chan_of // per == group_of).astype(F32)

    def compact(value, chosen):
        return jnp.dot(
            value, chosen, precision=lax.Precision.HIGHEST, preferred_element_type=F32
        )

    def spread(value):
        return lax.dot_general(
            value, members, (((1,), (1,)), ((), ())),
            precision=lax.Precision.HIGHEST, preferred_element_type=F32,
        )

    def add_up(fn):
        rows = []
        for b in range(2):
            total = None
            for f in range(3):
                part = jnp.sum(fn(2 * f + b, b), axis=0, keepdims=True)
                total = part if total is None else total + part
            rows.append(total)
        return jnp.concatenate(rows, axis=0)

    own_mean = group_total(add_up(lambda s, b: hid[s].astype(F32)), per) * (1.0 / local_count)

    def deviation(s, b):
        apart = hid[s].astype(F32) - own_mean[b : b + 1]
        return apart * apart

    own_square = group_total(add_up(deviation), per)
    zeros = jnp.zeros((4, own_mean.shape[1]), F32)
    local[0] = compact(jnp.concatenate([own_mean, own_square, zeros], axis=0), picks)
    pl.semaphore_wait(barrier, 30)
    for load in loads[:5] + loads[11:]:
        load.wait()
    def merge_rows():
        exchange_finish(0)
        mean, square = merge(0, float(local_count))
        local[1] = jnp.concatenate([mean, square, jnp.zeros((4, 128), F32)], axis=0)
        exchange_start(1)

    def merge_all():
        exchange_finish(1)
        mean, square = merge(1, float(local_count) * 16)
        rstd = lax.rsqrt(square * (1.0 / count) + EPS)
        both = jnp.concatenate([mean, rstd, jnp.zeros((4, 128), F32)], axis=0)
        moments[...] = spread(both)

    def prepare(s):
        b = s % 2
        mean, rstd = moments[b : b + 1], moments[2 + b : 3 + b]
        unit = (hid[s].astype(F32) - mean) * rstd
        pre = unit * gain_ref[...] + shift_ref[...]
        sig = 1.0 / (1.0 + jnp.exp(-pre))
        normed[s] = unit
        scale[s] = sig * (1.0 + pre * (1.0 - sig)) * gain_ref[...]

    def start_frames():
        for f in range(2):
            for b in range(2):
                frame_copy(f, b).start()

    def start_stats():
        exchange_start(0)

    def work(k, m):
        if m == 0:
            settle(k)
        matmul_half(m, tap(k) // 3, lax.rem(tap(k), 3))

    def work_planes(n, m):
        if m == 0:
            settle_planes(n)
        matmul_half(m, other_tap(n) // 3, lax.rem(other_tap(n), 3))

    steps = {
        "A": stage_1, "B": stage_2, "C": stage_3, "D": stage_4, "T": take_planes,
        "F": start_frames, "H": start_rows, "I": finish_rows, "J": finish_frames,
        "K": finish_corner, "E": start_stats, "M": merge_rows, "N": merge_all, "P": prepare,
        "W": work, "V": work_planes, "X": fold_columns,
    }
    for step in SCHEDULE:
        steps[step[0]](*(int(digit) for digit in step[1:]))
    settle(4)

    sums = [[None, None], [None, None]]
    for m in range(2):
        whole = acc[1, 3 * m : 3 * m + 3] + product(m, 1, 1)
        for i in range(3):
            s = 3 * m + i
            grad = whole[i] * scale[s]
            acc[1, s] = grad
            for kind, value in enumerate((grad, grad * normed[s])):
                part = jnp.sum(value, axis=0, keepdims=True)
                held = sums[kind][s % 2]
                sums[kind][s % 2] = part if held is None else held + part
    first, second = (jnp.concatenate(pair, axis=0) for pair in sums)
    local[2] = compact(jnp.concatenate([first, second, zeros], axis=0), members)
    exchange_start(2)

    for k in range(5):
        for slot in range(3):
            first_copy(k, slot).wait_send()
        for slot in range(2):
            second_copy(k, slot).wait_send()
        onward_copy(k).wait_send()
        for slot in range(4):
            core_copy(k, slot, core).wait_send()
    for n in range(SHARED):
        for slot in range(4):
            for end in range(2):
                plane_copy(n, slot, end).wait_send()
            pass_copy(n, slot, core).wait_send()
    @pl.when(core == 1)
    def _():
        for side in range(2):
            wing_copy(side).wait_send()
            for f in range(2):
                corner_copy(side, f).wait_send()

    for f in range(3):
        for side in range(2):
            for b in range(2):
                row_copy(side, f, b).wait_send()
        if f < 2:
            for b in range(2):
                frame_copy(f, b).wait_send()

    exchange_finish(2)
    local[3] = functools.reduce(jnp.add, [gathered[2, i] for i in range(16)])
    exchange_start(3)

    def sent(k, carry):
        for e in range(4):
            exchange_copy(e, k).wait_send()
        return carry

    lax.fori_loop(1, 16, sent, 0)
    exchange_finish(3)
    totals = functools.reduce(jnp.add, [gathered[3, i] for i in range(16)])
    means = spread(totals * (1.0 / count))

    stores = []
    for s in range(6):
        f, b = s // 2, s % 2
        rstd = moments[2 + b : 3 + b]
        low, slope = rstd * means[b : b + 1], rstd * means[2 + b : 3 + b]
        value = rstd * acc[1, s] - low - normed[s] * slope
        result[s] = value.astype(result.dtype)
        store = pltpu.make_async_copy(result.at[s], out_hbm.at[b, f, 0], out_sem.at[s])
        store.start()
        stores.append(store)

    for store in stores:
        store.wait()


def shards(hidden_state, grad_out, norm_gain, norm_shift, conv_weight):
    clips, frames, rows, width, chan = hidden_state.shape
    devices = lax.axis_size("tm") * lax.axis_size("row")
    count = clips * frames * rows * width * chan // clips // GROUPS * devices
    taps = jnp.swapaxes(conv_weight, 0, 1).reshape(3, 9, 2, 16, chan)
    bf16 = jnp.bfloat16
    anywhere = pl.BlockSpec(memory_space=pl.ANY)
    vmem = pl.BlockSpec(memory_space=pltpu.VMEM)
    dma = pltpu.SemaphoreType.DMA
    return pl.pallas_call(
        functools.partial(kernel, count),
        out_shape=jax.ShapeDtypeStruct(hidden_state.shape, bf16),
        in_specs=[anywhere, anywhere, vmem, vmem, anywhere],
        out_specs=anywhere,
        scratch_shapes=[
            pltpu.VMEM((3, 9, 4, 4, 2, 16, chan), bf16),
            pltpu.VMEM((3, 10, width, chan), bf16),
            pltpu.VMEM((3, 6, width, chan), F32),
            pltpu.VMEM((6, width, chan), bf16),
            pltpu.VMEM((6, width, chan), F32),
            pltpu.VMEM((6, width, chan), F32),
            pltpu.VMEM((6, width, chan), bf16),
            pltpu.VMEM((4, 8, 128), F32),
            pltpu.VMEM((4, 16, 8, 128), F32),
            pltpu.VMEM((8, chan), F32),
            dma((5, 10)), dma((5, 10)),
            dma((4, 4, 3)), dma((4, 4, 3)),
            dma((2, 6)), dma((2, 6)),
            dma((4,)), dma((4,)),
            dma((2, 2)), dma((2, 2)),
            dma((2,)), dma((2,)),
            dma((4, 16)), dma((4, 16)),
            dma((18,)), dma((6,)),
        ],
        compiler_params=pltpu.CompilerParams(
            collective_id=0, has_side_effects=True, vmem_limit_bytes=56 << 20
        ),
        name="conv_grad",
    )(hidden_state, grad_out, norm_gain.reshape(1, chan), norm_shift.reshape(1, chan), taps)


def solution(mesh):
    return jax.shard_map(
        shards,
        mesh=mesh,
        in_specs=(
            P(None, "tm", "row", None, None),
            P(None, "tm", "row", None, None),
            P(),
            P(),
            P("row", None, None),
        ),
        out_specs=P(None, "tm", "row", None, None),
        check_vma=False,
    )
```

```python
import functools

import jax
import jax.numpy as jnp
from jax import lax
from jax.experimental import pallas as pl
from jax.experimental.pallas import tpu as pltpu
from jax.sharding import PartitionSpec as P

GROUPS = 32
MESH = pl.DeviceIdType.MESH
F32 = jnp.float32
ITEMS = ((3, 5, True), (0, 2, False), (6, 8, True), (1, 7, True), (4, 4, False))
SCHEDULE = (
    "F", "A0", "A1", "A2", "A3", "A4", "E", "B0", "H00", "B1", "C0", "H01", "H10", "M", "B2",
    "C1", "D0", "H11", "H20", "J", "N", "B3", "C2", "D1", "H21", "P0", "P1", "P2", "T00", "W00",
    "P3", "W01", "I0", "I1", "B4", "C3", "D2", "P4", "T01", "P5", "T10", "T02", "V00", "V01",
    "C4", "D3", "T11", "I2", "K1", "W10", "W11", "T20", "T12", "K0", "W20", "W21", "D4", "T30",
    "T21", "V10", "T22", "V11", "W30", "T31", "W31", "V20", "T32", "V21", "X", "V30", "V31",
)
SHARED = 4
EPS = 1e-06


def group_total(value, per):
    lane = lax.broadcasted_iota(jnp.int32, value.shape, 1)
    size = value.shape[1]
    step = 1
    while step < per:
        other = jnp.where(
            (lane & step) != 0, pltpu.roll(value, step, 1), pltpu.roll(value, size - step, 1)
        )
        value = value + other
        step *= 2
    return value


def kernel(
    count,
    hid_hbm, cot_hbm, gain_ref, shift_ref, wt_hbm, out_hbm,
    kern, cot, acc, hid, normed, scale, result, local, gathered, moments,
    w_send, w_recv, z_send, z_recv, h_send, h_recv, f_send, f_recv, c_send, c_recv, v_send, v_recv,
    x_send, x_recv, load_sem, out_sem,
):
    tm, row = lax.axis_index("tm"), lax.axis_index("row")
    core = lax.rem(tm, 2)
    px, py = row // 4, lax.rem(row, 4)
    way = 1 - 2 * core
    x_way = jnp.where(py == 3, -1, jnp.where(py == 0, 1, way))
    odd = lax.rem(tm // 2, 2)
    per = gain_ref.shape[1] // GROUPS
    local_count = 3 * 160 * per

    def wrap(value, size):
        return lax.rem(value + size, size)

    def at_row(value):
        return (tm, wrap(value, 16))

    def at_tm(value):
        return (wrap(value, 16), row)

    def at_xy(x, y):
        return (tm, wrap(x, 4) * 4 + wrap(y, 4))

    partner = (tm + way, row)

    def remote(src, dst, send, recv, target):
        return pltpu.make_async_remote_copy(
            src_ref=src, dst_ref=dst, send_sem=send, recv_sem=recv,
            device_id=target, device_id_type=MESH,
        )

    def tap(k):
        even, other, _ = ITEMS[k]
        return even + odd * (other - even)

    def other_tap(n):
        even, other, _ = ITEMS[n]
        return other + odd * (even - other)

    def along(k, step):
        return at_xy(px, py + step) if ITEMS[k][2] else at_xy(px + step, py)

    def across(k, step):
        return at_xy(px + step, py) if ITEMS[k][2] else at_xy(px, py + step)

    def piece(k, step, half):
        x, y = (px, wrap(py + step, 4)) if ITEMS[k][2] else (wrap(px + step, 4), py)
        return kern.at[:, tap(k), x, y, half]

    def block(k, step, half, chosen=None):
        chosen = tap(k) if chosen is None else chosen
        if ITEMS[k][2]:
            return kern.at[:, chosen, wrap(px + step, 4), :, half]
        return kern.at[:, chosen, :, wrap(py + step, 4), half]

    def first_copy(k, slot):
        step = (1, -1, 2)[slot]
        return remote(
            wt_hbm.at[:, tap(k), core], piece(k, 0, core),
            w_send.at[k, slot], w_recv.at[k, slot], along(k, step),
        )

    def first_arrival(k, slot):
        step = (1, -1, 2)[slot]
        mine = piece(k, -step, core)
        return remote(mine, mine, w_send.at[k, slot], w_recv.at[k, slot], along(k, step))

    def second_copy(k, slot):
        step = (1, -1)[slot]
        mine = block(k, 0, core)
        return remote(mine, mine, w_send.at[k, 3 + slot], w_recv.at[k, 3 + slot], across(k, step))

    def second_arrival(k, slot):
        step = (1, -1)[slot]
        mine = block(k, -step, core)
        return remote(mine, mine, w_send.at[k, 3 + slot], w_recv.at[k, 3 + slot], across(k, step))

    def onward_copy(k):
        step = x_way if ITEMS[k][2] else way
        mine = block(k, -step, core)
        return remote(mine, mine, w_send.at[k, 5], w_recv.at[k, 5], across(k, step))

    def onward_arrival(k):
        mine = block(k, 2, core)
        return remote(mine, mine, w_send.at[k, 5], w_recv.at[k, 5], across(k, way))

    STEPS = (0, -1, 1, 2)

    def core_copy(k, slot, half):
        mine = block(k, STEPS[slot], half)
        return remote(mine, mine, w_send.at[k, 6 + slot], w_recv.at[k, 6 + slot], partner)

    def share(n, slot, end, chosen=None):
        k = n
        chosen = tap(k) if chosen is None else chosen
        there = pl.ds(2 * end, 2)
        if ITEMS[k][2]:
            return kern.at[:, chosen, wrap(px + STEPS[slot], 4), there, core]
        return kern.at[:, chosen, there, wrap(py + STEPS[slot], 4), core]

    def plane_copy(n, slot, end):
        mine = share(n, slot, end)
        return remote(
            mine, mine, z_send.at[n, slot, end], z_recv.at[n, slot, end],
            at_tm(tm + (2, -2)[end]),
        )

    def plane_arrival(n, slot, end):
        mine = share(n, slot, end, other_tap(n))
        return remote(mine, mine, z_send.at[n, slot, end], z_recv.at[n, slot, end], partner)

    def pass_copy(n, slot, half):
        mine = block(n, STEPS[slot], half, other_tap(n))
        return remote(mine, mine, z_send.at[n, slot, 2], z_recv.at[n, slot, 2], partner)

    def stage_1(k):
        for slot in (2, 0, 1):
            first_copy(k, slot).start()

    def hand_on(k, slot):
        if k < SHARED:
            for end in range(2):
                plane_copy(k, slot, end).start()
        core_copy(k, slot, core).start()

    def stage_2(k):
        for slot in range(3):
            first_arrival(k, slot).wait_recv()
        for slot in range(2):
            second_copy(k, slot).start()
        hand_on(k, 0)

    def stage_3(k):
        for slot in range(2):
            second_arrival(k, slot).wait_recv()
        onward_copy(k).start()
        for slot in range(2):
            hand_on(k, 1 + slot)

    def stage_4(k):
        onward_arrival(k).wait_recv()
        hand_on(k, 3)

    def take_planes(n, part):
        for slot in ((0,), (1, 2), (3,))[part]:
            for end in range(2):
                plane_arrival(n, slot, end).wait_recv()
            pass_copy(n, slot, core).start()

    def settle(k):
        for slot in range(4):
            core_copy(k, slot, 1 - core).wait_recv()

    def settle_planes(n):
        for slot in range(4):
            pass_copy(n, slot, 1 - core).wait_recv()

    def row_copy(side, f, b):
        step = (1, -1)[side]
        return remote(
            cot_hbm.at[b, f, 0], cot.at[2 * side, 2 * f + b],
            h_send.at[side, 2 * f + b], h_recv.at[side, 2 * f + b], at_row(row + step),
        )

    def frame_copy(f, b):
        return remote(
            cot_hbm.at[b, f, 0], cot.at[1, 6 + 2 * f + b],
            f_send.at[2 * f + b], f_recv.at[2 * f + b], at_tm(tm - 1),
        )

    def corner_copy(side, f):
        return remote(
            cot.at[2 * side, pl.ds(2 * f, 2)], cot.at[2 * side, pl.ds(6 + 2 * f, 2)],
            c_send.at[side, f], c_recv.at[side, f], partner,
        )

    def wing_copy(side):
        return remote(
            cot.at[1, pl.ds(6, 4)], cot.at[2 * side, pl.ds(6, 4)],
            v_send.at[side], v_recv.at[side], at_row(row + (1, -1)[side]),
        )

    def start_rows(f, b):
        for side in range(2):
            row_copy(side, f, b).start()

    def finish_rows(f):
        for side in range(2):
            for b in range(2):
                row_copy(side, f, b).wait_recv()

            @pl.when(row == (0, 15)[side])
            def _():
                cot[2 * side, pl.ds(2 * f, 2)] = jnp.zeros((2, 160, 512), cot.dtype)

            if f < 2:

                @pl.when(core == 1)
                def _():
                    corner_copy(side, f).start()

    def finish_corner(side):
        @pl.when(core == 0)
        def _():
            for f in range(2):
                corner_copy(side, f).wait_recv()

        @pl.when(core == 1)
        def _():
            wing_copy(side).wait_recv()

        @pl.when(row == (0, 15)[side])
        def _():
            cot[2 * side, pl.ds(6, 4)] = jnp.zeros((4, 160, 512), cot.dtype)

    def finish_frames():
        for f in range(2):
            for b in range(2):
                frame_copy(f, b).wait_recv()

        @pl.when(tm == 15)
        def _():
            cot[1, pl.ds(6, 4)] = jnp.zeros((4, 160, 512), cot.dtype)

        @pl.when(core == 1)
        def _():
            for side in range(2):
                wing_copy(side).start()

    def exchange_copy(e, k):
        if e % 2 == 0:
            me, target = row, at_row(row + k)
        else:
            me, target = tm, at_tm(tm + k)
        return remote(local.at[e], gathered.at[e, me], x_send.at[e, k], x_recv.at[e, me], target)

    def exchange_start(e):
        me = row if e % 2 == 0 else tm
        gathered[e, me] = local[e]

        def body(k, carry):
            exchange_copy(e, k).start()
            return carry

        lax.fori_loop(1, 16, body, 0)

    def exchange_finish(e):
        me = row if e % 2 == 0 else tm

        def body(k, carry):
            other = lax.rem(me + k, 16)
            there = gathered.at[e, other]
            remote(there, there, x_send.at[e, k], x_recv.at[e, other], partner).wait_recv()
            return carry

        lax.fori_loop(1, 16, body, 0)

    def merge(e, each):
        stats = [gathered[e, i] for i in range(16)]
        mean = functools.reduce(jnp.add, [s[0:2] for s in stats]) * (1.0 / 16)
        square = functools.reduce(jnp.add, [s[2:4] for s in stats])
        for s in stats:
            apart = s[0:2] - mean
            square = square + each * (apart * apart)
        return mean, square

    def product(m, kr, kw):
        total = None
        for kt in range(3):
            lhs = cot[2 - kr, pl.ds(2 * (2 - kt) + 3 * m, 3)].reshape(480, 512)
            rhs = kern[kt, 3 * kr + kw].reshape(512, 512)
            part = lax.dot_general(
                lhs, rhs, (((1,), (1,)), ((), ())), preferred_element_type=F32
            )
            total = part if total is None else total + part
        return total.reshape(3, 160, 512)

    def matmul_half(m, kr, kw):
        here = pl.ds(3 * m, 3)
        acc[kw, here] = acc[kw, here] + product(m, kr, kw)

    def fold_columns():
        def body(s, carry):
            place = lax.broadcasted_iota(jnp.int32, (160, 512), 0)
            later = jnp.where(place < 159, pltpu.roll(acc[0, s], 159, 0), 0.0)
            earlier = jnp.where(place > 0, pltpu.roll(acc[2, s], 1, 0), 0.0)
            acc[1, s] = acc[1, s] + later + earlier
            return carry

        lax.fori_loop(0, 6, body, 0)

    barrier = pltpu.get_barrier_semaphore()

    def greet(k, carry):
        pl.semaphore_signal(barrier, inc=1, device_id=at_row(row + k), device_id_type=MESH)
        pl.semaphore_signal(barrier, inc=1, device_id=at_tm(tm + k), device_id_type=MESH)
        return carry

    lax.fori_loop(1, 16, greet, 0)

    loads = [
        pltpu.make_async_copy(wt_hbm.at[:, tap(k), core], piece(k, 0, core), load_sem.at[13 + k])
        for k in range(5)
    ]
    for f in range(3):
        for b in range(2):
            s = 2 * f + b
            loads.append(
                pltpu.make_async_copy(hid_hbm.at[b, f, 0], hid.at[s], load_sem.at[1 + s])
            )
    for f in range(3):
        for b in range(2):
            s = 2 * f + b
            loads.append(
                pltpu.make_async_copy(cot_hbm.at[b, f, 0], cot.at[1, s], load_sem.at[7 + s])
            )
    for load in loads:
        load.start()
    acc[...] = jnp.zeros_like(acc)

    for load in loads[5:11]:
        load.wait()

    chan_of = lax.broadcasted_iota(jnp.int32, (512, 128), 0)
    group_of = lax.broadcasted_iota(jnp.int32, (512, 128), 1)
    picks = (chan_of == group_of * per).astype(F32)
    members = (chan_of // per == group_of).astype(F32)

    def compact(value, chosen):
        return jnp.dot(
            value, chosen, precision=lax.Precision.HIGHEST, preferred_element_type=F32
        )

    def spread(value):
        return lax.dot_general(
            value, members, (((1,), (1,)), ((), ())),
            precision=lax.Precision.HIGHEST, preferred_element_type=F32,
        )

    def add_up(fn):
        rows = []
        for b in range(2):
            total = None
            for f in range(3):
                part = jnp.sum(fn(2 * f + b, b), axis=0, keepdims=True)
                total = part if total is None else total + part
            rows.append(total)
        return jnp.concatenate(rows, axis=0)

    own_mean = group_total(add_up(lambda s, b: hid[s].astype(F32)), per) * (1.0 / local_count)

    def deviation(s, b):
        apart = hid[s].astype(F32) - own_mean[b : b + 1]
        return apart * apart

    own_square = group_total(add_up(deviation), per)
    zeros = jnp.zeros((4, own_mean.shape[1]), F32)
    local[0] = compact(jnp.concatenate([own_mean, own_square, zeros], axis=0), picks)
    pl.semaphore_wait(barrier, 30)
    for load in loads[:5] + loads[11:]:
        load.wait()
    def merge_rows():
        exchange_finish(0)
        mean, square = merge(0, float(local_count))
        local[1] = jnp.concatenate([mean, square, jnp.zeros((4, 128), F32)], axis=0)
        exchange_start(1)

    def merge_all():
        exchange_finish(1)
        mean, square = merge(1, float(local_count) * 16)
        rstd = lax.rsqrt(square * (1.0 / count) + EPS)
        both = jnp.concatenate([mean, rstd, jnp.zeros((4, 128), F32)], axis=0)
        moments[...] = spread(both)

    def prepare(s):
        b = s % 2
        mean, rstd = moments[b : b + 1], moments[2 + b : 3 + b]
        unit = (hid[s].astype(F32) - mean) * rstd
        pre = unit * gain_ref[...] + shift_ref[...]
        sig = 1.0 / (1.0 + jnp.exp(-pre))
        normed[s] = unit
        scale[s] = sig * (1.0 + pre * (1.0 - sig)) * gain_ref[...]

    def start_frames():
        for f in range(2):
            for b in range(2):
                frame_copy(f, b).start()

    def start_stats():
        exchange_start(0)

    def work(k, m):
        if m == 0:
            settle(k)
        matmul_half(m, tap(k) // 3, lax.rem(tap(k), 3))

    def work_planes(n, m):
        if m == 0:
            settle_planes(n)
        matmul_half(m, other_tap(n) // 3, lax.rem(other_tap(n), 3))

    steps = {
        "A": stage_1, "B": stage_2, "C": stage_3, "D": stage_4, "T": take_planes,
        "F": start_frames, "H": start_rows, "I": finish_rows, "J": finish_frames,
        "K": finish_corner, "E": start_stats, "M": merge_rows, "N": merge_all, "P": prepare,
        "W": work, "V": work_planes, "X": fold_columns,
    }
    for step in SCHEDULE:
        steps[step[0]](*(int(digit) for digit in step[1:]))
    settle(4)

    sums = [[None, None], [None, None]]
    for m in range(2):
        whole = acc[1, 3 * m : 3 * m + 3] + product(m, 1, 1)
        for i in range(3):
            s = 3 * m + i
            grad = whole[i] * scale[s]
            acc[1, s] = grad
            for kind, value in enumerate((grad, grad * normed[s])):
                part = jnp.sum(value, axis=0, keepdims=True)
                held = sums[kind][s % 2]
                sums[kind][s % 2] = part if held is None else held + part
    first, second = (jnp.concatenate(pair, axis=0) for pair in sums)
    local[2] = compact(jnp.concatenate([first, second, zeros], axis=0), members)
    exchange_start(2)

    for k in range(5):
        for slot in range(3):
            first_copy(k, slot).wait_send()
        for slot in range(2):
            second_copy(k, slot).wait_send()
        onward_copy(k).wait_send()
        for slot in range(4):
            core_copy(k, slot, core).wait_send()
    for n in range(SHARED):
        for slot in range(4):
            for end in range(2):
                plane_copy(n, slot, end).wait_send()
            pass_copy(n, slot, core).wait_send()
    @pl.when(core == 1)
    def _():
        for side in range(2):
            wing_copy(side).wait_send()
            for f in range(2):
                corner_copy(side, f).wait_send()

    for f in range(3):
        for side in range(2):
            for b in range(2):
                row_copy(side, f, b).wait_send()
        if f < 2:
            for b in range(2):
                frame_copy(f, b).wait_send()

    exchange_finish(2)
    local[3] = functools.reduce(jnp.add, [gathered[2, i] for i in range(16)])
    exchange_start(3)

    def sent(k, carry):
        for e in range(4):
            exchange_copy(e, k).wait_send()
        return carry

    lax.fori_loop(1, 16, sent, 0)
    exchange_finish(3)
    totals = functools.reduce(jnp.add, [gathered[3, i] for i in range(16)])
    means = spread(totals * (1.0 / count))

    stores = []
    for s in range(6):
        f, b = s // 2, s % 2
        rstd = moments[2 + b : 3 + b]
        low, slope = rstd * means[b : b + 1], rstd * means[2 + b : 3 + b]
        value = rstd * acc[1, s] - low - normed[s] * slope
        result[s] = value.astype(result.dtype)
        store = pltpu.make_async_copy(result.at[s], out_hbm.at[b, f, 0], out_sem.at[s])
        store.start()
        stores.append(store)

    for store in stores:
        store.wait()


def shards(hidden_state, grad_out, norm_gain, norm_shift, conv_weight):
    clips, frames, rows, width, chan = hidden_state.shape
    devices = lax.axis_size("tm") * lax.axis_size("row")
    count = clips * frames * rows * width * chan // clips // GROUPS * devices
    taps = jnp.swapaxes(conv_weight, 0, 1).reshape(3, 9, 2, 16, chan)
    bf16 = jnp.bfloat16
    anywhere = pl.BlockSpec(memory_space=pl.ANY)
    vmem = pl.BlockSpec(memory_space=pltpu.VMEM)
    dma = pltpu.SemaphoreType.DMA
    return pl.pallas_call(
        functools.partial(kernel, count),
        out_shape=jax.ShapeDtypeStruct(hidden_state.shape, bf16),
        in_specs=[anywhere, anywhere, vmem, vmem, anywhere],
        out_specs=anywhere,
        scratch_shapes=[
            pltpu.VMEM((3, 9, 4, 4, 2, 16, chan), bf16),
            pltpu.VMEM((3, 10, width, chan), bf16),
            pltpu.VMEM((3, 6, width, chan), F32),
            pltpu.VMEM((6, width, chan), bf16),
            pltpu.VMEM((6, width, chan), F32),
            pltpu.VMEM((6, width, chan), F32),
            pltpu.VMEM((6, width, chan), bf16),
            pltpu.VMEM((4, 8, 128), F32),
            pltpu.VMEM((4, 16, 8, 128), F32),
            pltpu.VMEM((8, chan), F32),
            dma((5, 10)), dma((5, 10)),
            dma((4, 4, 3)), dma((4, 4, 3)),
            dma((2, 6)), dma((2, 6)),
            dma((4,)), dma((4,)),
            dma((2, 2)), dma((2, 2)),
            dma((2,)), dma((2,)),
            dma((4, 16)), dma((4, 16)),
            dma((18,)), dma((6,)),
        ],
        compiler_params=pltpu.CompilerParams(
            collective_id=0, has_side_effects=True, vmem_limit_bytes=56 << 20
        ),
        name="conv_grad",
    )(hidden_state, grad_out, norm_gain.reshape(1, chan), norm_shift.reshape(1, chan), taps)


def solution(mesh):
    return jax.shard_map(
        shards,
        mesh=mesh,
        in_specs=(
            P(None, "tm", "row", None, None),
            P(None, "tm", "row", None, None),
            P(),
            P(),
            P("row", None, None),
        ),
        out_specs=P(None, "tm", "row", None, None),
        check_vma=False,
    )
```
